512 devices in a mesh: leaf: 16 (over y, x), src: 32 (over z, core).
Axes of the slice: x: 4, y: 4, z: 16, core: 2. Of those that a mesh axis runs over, the one named last changes fastest.
Arguments:
- leaf_rhs: float32 [16, 8192, 1024], P('leaf', 'src'), may hold values from -6 to 6
- leaf_factor: float32 [16, 1536, 1024], P('leaf', 'src'), may hold values from -0.1875 to 0.1875
- pivot_count: int32 [16], P('leaf'), may hold values from 128 to 1024, as said below
- parent: int32 [16], replicated, may hold values from 0 to 3, as said below
- leaf_index: int32 [16, 512], replicated, may hold values from 0 to 1023, as said below
- separator_rhs: float32 [16, 512, 4, 512], P('leaf', 'src'), may hold values from -6 to 6
- separator_factor: float32 [4, 1024, 512], P(None, 'src'), may hold values from -0.25 to 0.25
- separator_index: int32 [4, 512], replicated, may hold values from 0 to 511, as said below
- root_rhs: float32 [16, 512, 512], P('leaf', 'src'), may hold values from -6 to 6
- root_factor: float32 [512, 512], P('src'), may hold values from -0.25 to 0.25
Outputs:
- leaf_solution: float32 [16, 8192, 1024], P('leaf', 'src')
- separator_solution: float32 [16, 512, 4, 512], P('leaf', 'src')
- root_solution: float32 [16, 512, 512], P('leaf', 'src')
The draws below stay inside these ranges and needn't reach their ends.
Inputs may be any that keep to these rules, and one draw needn't show every extreme that they name: Every separator is the parent of exactly 4 leaves. `pivot_count`: multiples of 128. `leaf_index`: each row holds distinct values. `separator_index`: each row holds distinct values.
All inputs are finite; a program needn't handle non-finite values.
Results may differ from the reference program's by a relative error of at most 0.0003.
Values sent between devices are 32-bit elements; how exact they have to be, the bound alone decides.
No kernel may reach another device: no remote copies, remote signals or barrier semaphores. Data moves between devices by JAX's collectives and lax.ppermute only.
A program may use at most 128 MiB of HBM per device.

```python
import jax
import jax.numpy as jnp
from jax import lax

PIV = 1024
BORD = 512
SEP_PIV = 512
SEP_BORD = 512
ROOT_PIV = 512
BLOCK = 128
COLS = 256
LEAVES = 16
SEPS = 4
RHS = 8192
N_LEAF = 16
N_SRC = 32


def draw_parent(key, part):
    key = jax.random.fold_in(key, 11)
    shuffled = jax.random.permutation(key, LEAVES)
    return (shuffled // (LEAVES // SEPS)).astype(jnp.int32)


def draw_pivot_count(key, part):
    key = jax.random.fold_in(key, 12)
    first_key, second_key = jax.random.split(key)
    counts_drawn = BLOCK * jax.random.randint(first_key, (LEAVES,), 1, PIV // BLOCK + 1)
    shuffled = jax.random.permutation(second_key, LEAVES)
    counts_drawn = counts_drawn.at[shuffled[0]].set(PIV).at[shuffled[1]].set(BLOCK)
    return counts_drawn.astype(jnp.int32)


def distinct_rows(key, how_many, chosen, extent):
    keys_all = jax.random.split(key, how_many)
    rows_all = jax.vmap(lambda single: jax.random.permutation(single, extent)[:chosen])(keys_all)
    leading = jnp.concatenate([jax.random.permutation(keys_all[0], extent - 1)[:chosen - 1], jnp.full((1,), extent - 1, rows_all.dtype)])
    return rows_all.at[0].set(leading).astype(jnp.int32)


def draw_leaf_index(key, part):
    key = jax.random.fold_in(key, 13)
    return distinct_rows(key, LEAVES, BORD, SEP_PIV + SEP_BORD)


def draw_separator_index(key, part):
    key = jax.random.fold_in(key, 14)
    return distinct_rows(key, SEPS, SEP_BORD, ROOT_PIV)


def levels(own_key, dims, shards, smallest, high):
    factor_of, own = 1.0, jax.random.fold_in(own_key, 6)
    for axis_at, parts in shards:
        steps = jnp.exp(jax.random.uniform(jax.random.fold_in(own, axis_at), (parts,), jnp.float32, smallest / len(shards), high / len(shards)))
        factor_of = factor_of * jnp.repeat(steps, dims[axis_at] // parts).reshape([-1 if axis == axis_at else 1 for axis in range(len(dims))])
    return factor_of


def noise(own_key, shape, scale, bound, shards=(), kind=jnp.bfloat16):
    factor_of = levels(own_key, shape, shards, -0.22, 0.18) if shards else 1.0
    array = jax.random.normal(own_key, shape, jnp.float32) * scale * factor_of
    return jnp.minimum(jnp.maximum(array, -bound), bound).astype(kind)


def setup_inputs(seed: int = 0) -> dict:
    arg_keys = jax.random.split(jax.random.key(seed), 11)
    leaf_rhs = noise(arg_keys[0], (LEAVES, RHS, PIV), 1.0, 6.0, ((0, 16), (1, 32)), jnp.float32)
    leaf_factor = noise(arg_keys[1], (LEAVES, PIV + BORD, PIV), PIV ** -0.5, 0.1875, ((0, 16), (1, 32)), jnp.float32)
    pivot_count = draw_pivot_count(jax.random.fold_in(arg_keys[10], 71), 0)
    parent = draw_parent(jax.random.fold_in(arg_keys[10], 71), 0)
    leaf_index = draw_leaf_index(jax.random.fold_in(arg_keys[10], 71), 0)
    separator_rhs = noise(arg_keys[5], (LEAVES, RHS // LEAVES, SEPS, SEP_PIV), 1.0, 6.0, ((0, 16), (1, 32)), jnp.float32)
    separator_factor = noise(arg_keys[6], (SEPS, SEP_PIV + SEP_BORD, SEP_PIV), SEP_PIV ** -0.5, 0.25, ((1, 32),), jnp.float32)
    separator_index = draw_separator_index(jax.random.fold_in(arg_keys[10], 71), 0)
    root_rhs = noise(arg_keys[8], (LEAVES, RHS // LEAVES, ROOT_PIV), 1.0, 6.0, ((0, 16), (1, 32)), jnp.float32)
    root_factor = noise(arg_keys[9], (ROOT_PIV, ROOT_PIV), ROOT_PIV ** -0.5, 0.25, ((0, 32),), jnp.float32)
    return {"leaf_rhs": leaf_rhs, "leaf_factor": leaf_factor, "pivot_count": pivot_count, "parent": parent, "leaf_index": leaf_index, "separator_rhs": separator_rhs, "separator_factor": separator_factor, "separator_index": separator_index, "root_rhs": root_rhs, "root_factor": root_factor}


def front_matrix(block_rows, first_row, pivots, top_rows):
    row_ids = first_row + jnp.arange(block_rows.shape[0], dtype=jnp.int32)[:, None]
    col_ids = jnp.arange(block_rows.shape[1], dtype=jnp.int32)[None, :]
    in_pivot = row_ids < top_rows
    within = jnp.where(in_pivot, (row_ids < pivots) & (col_ids < row_ids), True)
    keeper = (col_ids < pivots) & within
    diagonal = in_pivot & (col_ids == row_ids) & (col_ids < pivots)
    return jnp.where(keeper, block_rows, 0.0) + diagonal.astype(block_rows.dtype)


def against_rows(left_side, matrix):
    return lax.dot_general(left_side, matrix, (((1,), (1,)), ((), ())), precision=lax.Precision.HIGHEST, preferred_element_type=jnp.float32)


def against_cols(left_side, matrix):
    return jnp.dot(left_side, matrix, precision=lax.Precision.HIGHEST, preferred_element_type=jnp.float32)


def reference(leaf_rhs, leaf_factor, pivot_count, parent, leaf_index, separator_rhs, separator_factor, separator_index, root_rhs, root_factor):
    block_cols = COLS // N_LEAF
    sep_height = SEP_PIV + SEP_BORD
    sep_natural = separator_rhs.reshape(N_LEAF, N_SRC, block_cols, SEPS, SEP_PIV).transpose(3, 1, 0, 2, 4).reshape(SEPS, RHS, SEP_PIV)
    root_natural = root_rhs.reshape(N_LEAF, N_SRC, block_cols, ROOT_PIV).transpose(1, 0, 2, 3).reshape(RHS, ROOT_PIV)

    def leaf_forward(packed):
        right_side, factor, pivots = packed
        return against_rows(right_side, front_matrix(factor, 0, pivots, PIV))

    forward = lax.map(leaf_forward, (leaf_rhs, leaf_factor, pivot_count))
    leaf_solved = forward[:, :, :PIV]
    leaf_border = forward[:, :, PIV:]
    updates = jnp.zeros((SEPS, RHS, sep_height), jnp.float32)
    for leaf_number in range(LEAVES):
        spread = jnp.zeros((RHS, sep_height), jnp.float32).at[:, leaf_index[leaf_number]].add(leaf_border[leaf_number])
        chosen = (jnp.arange(SEPS, dtype=jnp.int32) == parent[leaf_number]).astype(jnp.float32)
        updates = updates + chosen[:, None, None] * spread[None]
    sep_operator = jax.vmap(lambda factor: front_matrix(factor, 0, SEP_PIV, SEP_PIV))(separator_factor)
    sep_pivot = sep_natural + updates[:, :, :SEP_PIV]
    sep_forward = jnp.einsum("jcp,jrp->jcr", sep_pivot, sep_operator, precision=lax.Precision.HIGHEST)
    sep_solved = sep_forward[:, :, :SEP_PIV]
    sep_border = sep_forward[:, :, SEP_PIV:] + updates[:, :, SEP_PIV:]
    root_total = root_natural
    for number in range(SEPS):
        root_total = root_total.at[:, separator_index[number]].add(sep_border[number])
    root_operator = front_matrix(root_factor, 0, ROOT_PIV, ROOT_PIV)
    root_solved = against_rows(root_total, root_operator)
    root_answer = against_cols(root_solved, root_operator)
    root_border = jnp.stack([root_answer[:, separator_index[number]] for number in range(SEPS)])
    sep_joined = jnp.concatenate([sep_solved, root_border], axis=2)
    sep_answer = jnp.einsum("jcr,jrp->jcp", sep_joined, sep_operator, precision=lax.Precision.HIGHEST)
    sep_full = jnp.concatenate([sep_answer, root_border], axis=2)

    def leaf_backward(packed):
        solved, factor, pivots, owner_sep, border_list = packed
        border = jnp.take(sep_full, owner_sep, axis=0)[:, border_list]
        joined = jnp.concatenate([solved, border], axis=1)
        return against_cols(joined, front_matrix(factor, 0, pivots, PIV))

    leaf_answer = lax.map(leaf_backward, (leaf_solved, leaf_factor, pivot_count, parent, leaf_index))
    sep_layout = sep_answer.reshape(SEPS, N_SRC, N_LEAF, block_cols, SEP_PIV).transpose(2, 1, 3, 0, 4).reshape(N_LEAF, N_SRC * block_cols, SEPS, SEP_PIV)
    root_layout = root_answer.reshape(N_SRC, N_LEAF, block_cols, ROOT_PIV).transpose(1, 0, 2, 3).reshape(N_LEAF, N_SRC * block_cols, ROOT_PIV)
    return leaf_answer, sep_layout, root_layout
```

```python
import jax
import jax.numpy as jnp
from jax import lax
from jax.experimental import pallas as pl
from jax.experimental.pallas import tpu as pltpu
from jax.sharding import Mesh, PartitionSpec as P

NY, NX, NZ, NC = 4, 4, 16, 2
F32, BF16 = jnp.float32, jnp.bfloat16
LANES = 128


def split2(value):
    high = value.astype(BF16)
    return high, (value - high.astype(F32)).astype(BF16)


def dot_nt(a, b):
    return lax.dot_general(a, b, (((1,), (1,)), ((), ())), preferred_element_type=F32)


def dot_nn(a, b):
    return lax.dot_general(a, b, (((1,), (0,)), ((), ())), preferred_element_type=F32)


def three_products(dot, a, b):
    return dot(a[0], b[0]) + (dot(a[1], b[0]) + dot(a[0], b[1]))


def stacked_products(dot, a, b):
    rows = a[0].shape[0]
    both = dot(jnp.concatenate([a[0], a[1]], axis=0), b[0])
    return both[:rows] + (both[rows:] + dot(a[0], b[1]))


def params(mebibytes):
    return pltpu.CompilerParams(vmem_limit_bytes=mebibytes * 1024 * 1024)


def full_vmem():
    return pl.BlockSpec(memory_space=pltpu.VMEM)


def full_smem():
    return pl.BlockSpec(memory_space=pltpu.SMEM)


def anywhere():
    return pl.BlockSpec(memory_space=pl.ANY)


def line_copies(c, own_ref, other_ref, buffer, shards, sem):
    first, last = shards
    copies = []
    for ref, parity in ((own_ref, c), (other_ref, 1 - c)):
        for z in range(first // 2, last // 2 + 1):
            shard = 2 * z + parity
            row = pl.multiple_of((shard - first) * 48, 16)
            at = z - (NZ - ref.shape[0])
            copies.append(((shard >= first) & (shard <= last), ref, at, row))

    def each(action):
        for wanted, ref, at, row in copies:
            @pl.when(wanted)
            def _():
                for half in range(2):
                    action(pltpu.make_async_copy(
                        ref.at[at, pl.ds(48 * half, 48), :],
                        buffer.at[pl.ds(row, 48), pl.ds(512 * half, 512)],
                        sem,
                    ))

    return each


def leaf_border_kernel(place_ref, count_ref, rhs_ref, own_ref, other_ref, border_ref, buffer, sem):
    each = line_copies(place_ref[0], own_ref, other_ref, buffer, (21, 31), sem)
    each(lambda copy: copy.start())
    cols = lax.broadcasted_iota(jnp.int32, rhs_ref.shape, 1)
    rhs = split2(jnp.where(cols < count_ref[0], rhs_ref[...], 0.0))
    each(lambda copy: copy.wait())
    for block in range(2):
        rows = split2(buffer[pl.ds(16 + 256 * block, 256), :])
        border_ref[:, 256 * block : 256 * (block + 1)] = three_products(dot_nt, rhs, rows)


def leaf_border(place, count, rhs, own, other):
    return pl.pallas_call(
        leaf_border_kernel,
        out_shape=jax.ShapeDtypeStruct((256, 512), F32),
        in_specs=[full_smem(), full_smem(), full_vmem(), anywhere(), anywhere()],
        out_specs=full_vmem(),
        scratch_shapes=[pltpu.VMEM((528, 1024), F32), pltpu.SemaphoreType.DMA],
        compiler_params=params(16),
        name="leaf_border",
    )(place, count, rhs, own, other)


def leaf_pivot_kernel(
    place_ref, count_ref, rhs_ref, own_ref, other_ref,
    part_ref, border_high_ref, border_low_ref,
    buffer, border_buffer, high_ref, low_ref, sem,
):
    c = place_ref[0]
    each = line_copies(c, own_ref, other_ref, buffer, (0, 21), sem.at[0])
    each_border = line_copies(c, own_ref, other_ref, border_buffer, (21, 31), sem.at[1])
    each(lambda copy: copy.start())
    each_border(lambda copy: copy.start())
    count = count_ref[0]
    cols = lax.broadcasted_iota(jnp.int32, rhs_ref.shape, 1)
    rhs = split2(jnp.where(cols < count, rhs_ref[...], 0.0))
    each(lambda copy: copy.wait())
    solved = []
    for block in range(4):
        first, wide = 256 * block, 256 * (block + 1)
        rows = first + lax.broadcasted_iota(jnp.int32, (256, wide), 0)
        columns = lax.broadcasted_iota(jnp.int32, (256, wide), 1)
        values = jnp.where(columns < rows, buffer[first:wide, :wide], 0.0)
        values = jnp.where(columns == rows, 1.0, values)
        values = jnp.where(rows < count, values, 0.0)
        high, low = split2(values)
        high_ref[first:wide, :wide] = high
        low_ref[first:wide, :wide] = low
        solved.append(three_products(dot_nt, (rhs[0][:, :wide], rhs[1][:, :wide]), (high, low)))
    solved = split2(jnp.concatenate(solved, axis=1))
    for block in range(4):
        first, wide = 256 * block, 256 * (block + 1)
        part_ref[:, first:wide] = three_products(
            dot_nn,
            (solved[0][:, first:], solved[1][:, first:]),
            (high_ref[first:, first:wide], low_ref[first:, first:wide]),
        )
    each_border(lambda copy: copy.wait())
    border_high_ref[...], border_low_ref[...] = split2(border_buffer[16:, :])


def leaf_pivot(place, count, rhs, own, other):
    return pl.pallas_call(
        leaf_pivot_kernel,
        out_shape=(
            jax.ShapeDtypeStruct((256, 1024), F32),
            jax.ShapeDtypeStruct((512, 1024), BF16),
            jax.ShapeDtypeStruct((512, 1024), BF16),
        ),
        in_specs=[full_smem(), full_smem(), full_vmem(), anywhere(), anywhere()],
        out_specs=(full_vmem(),) * 3,
        scratch_shapes=[
            pltpu.VMEM((1056, 1024), F32),
            pltpu.VMEM((528, 1024), F32),
            pltpu.VMEM((1024, 1024), BF16),
            pltpu.VMEM((1024, 1024), BF16),
            pltpu.SemaphoreType.DMA((2,)),
        ],
        compiler_params=params(24),
        name="leaf_pivot",
    )(place, count, rhs, own, other)


def leaf_last_kernel(count_ref, part_ref, border_ref, high_ref, low_ref, out_ref):
    border = split2(border_ref[...])
    answer = part_ref[...] + three_products(dot_nn, border, (high_ref[...], low_ref[...]))
    width = answer.shape[1]
    cols = pl.program_id(0) * width + lax.broadcasted_iota(jnp.int32, answer.shape, 1)
    out_ref[...] = jnp.where(cols < count_ref[0], answer, 0.0)


def leaf_last(count, part, border, high, low):
    width = 256
    return pl.pallas_call(
        leaf_last_kernel,
        out_shape=jax.ShapeDtypeStruct((256, 1024), F32),
        grid=(1024 // width,),
        in_specs=[
            full_smem(),
            pl.BlockSpec((256, width), lambda i: (0, i)),
            pl.BlockSpec((256, 512), lambda i: (0, 0)),
            pl.BlockSpec((512, width), lambda i: (0, i)),
            pl.BlockSpec((512, width), lambda i: (0, i)),
        ],
        out_specs=pl.BlockSpec((256, width), lambda i: (0, i)),
        compiler_params=params(12),
        name="leaf_last",
    )(count, part, border, high, low)


def pick(values, index_row):
    out = []
    for block in range(index_row.shape[1] // LANES):
        index = jnp.broadcast_to(index_row[:, block * LANES : (block + 1) * LANES], (16, LANES))
        lane, source = index & (LANES - 1), index >> 7
        total = jnp.zeros((16, LANES), F32)
        for at, value in enumerate(values):
            taken = jnp.take_along_axis(value, lane, axis=1)
            total = jnp.where(source == at, taken, total)
        out.append(total)
    return out


def blocks(value):
    return [value[:, at * LANES : (at + 1) * LANES] for at in range(value.shape[1] // LANES)]


def spread_kernel(parent_ref, incoming_ref, slot_ref, updates_ref):
    updates_ref[...] = jnp.zeros(updates_ref.shape, F32)

    def spread(leaf, _):
        to = parent_ref[leaf]
        picked = pick(blocks(incoming_ref[leaf]), slot_ref[leaf])
        for at, value in enumerate(picked):
            part = slice(at * LANES, (at + 1) * LANES)
            updates_ref[to, :, part] = updates_ref[to, :, part] + value
        return 0

    lax.fori_loop(0, 16, spread, 0)


def spread_updates(parent, incoming, slots):
    return pl.pallas_call(
        spread_kernel,
        out_shape=jax.ShapeDtypeStruct((4, 16, 1024), F32),
        in_specs=[full_smem(), full_vmem(), full_vmem()],
        out_specs=full_vmem(),
        compiler_params=params(8),
        name="spread_updates",
    )(parent, incoming, slots)


def lower_unit(value, row_ids, col_ids):
    return jnp.where(col_ids == row_ids, 1.0, jnp.where(col_ids < row_ids, value, 0.0))


def upper_kernel(
    place_ref, parent_ref, updates_ref, index_ref, sep_rhs_ref, sep_slot_ref, sep_index_ref, root_rhs_ref,
    own_ref, other_ref,
    down_ref, sep_out_ref, root_out_ref,
    solved, full, sep_buffer, root_buffer, high_ref, low_ref, sem,
):
    c = place_ref[0]
    loads = []
    for sep in range(4):
        rows = pl.ds(96 + 32 * sep, 32)
        loads.append([
            pltpu.make_async_copy(ref.at[:, rows, :], sep_buffer.at[sep, :, parity], sem.at[2 * sep + at])
            for at, (ref, parity) in enumerate(((own_ref, c), (other_ref, 1 - c)))
        ])
    loads.append([
        pltpu.make_async_copy(ref.at[:, pl.ds(224, 16), :], root_buffer.at[:, parity], sem.at[8 + at])
        for at, (ref, parity) in enumerate(((own_ref, c), (other_ref, 1 - c)))
    ])
    for pair in loads:
        for load in pair:
            load.start()
    row_ids = lax.broadcasted_iota(jnp.int32, (512, 512), 0)
    col_ids = lax.broadcasted_iota(jnp.int32, (512, 512), 1)
    root_total = root_rhs_ref[...]
    for sep in range(4):
        for load in loads[sep]:
            load.wait()
        top = lower_unit(sep_buffer[sep, :8].reshape(512, 512), row_ids, col_ids)
        high_ref[sep, :512], low_ref[sep, :512] = split2(top)
        high_ref[sep, 512:], low_ref[sep, 512:] = split2(sep_buffer[sep, 8:].reshape(512, 512))
        pivot = split2(sep_rhs_ref[sep] + updates_ref[sep, :, :512])
        forward = stacked_products(dot_nt, pivot, (high_ref[sep], low_ref[sep]))
        solved[sep] = forward[:, :512]
        border = forward[:, 512:] + updates_ref[sep, :, 512:]
        root_total = root_total + jnp.concatenate(pick(blocks(border), sep_slot_ref[sep]), axis=1)
    for load in loads[4]:
        load.wait()
    root = split2(lower_unit(root_buffer[...].reshape(512, 512), row_ids, col_ids))
    root_solved = stacked_products(dot_nt, split2(root_total), root)
    root_answer = stacked_products(dot_nn, split2(root_solved), root)
    root_out_ref[...] = root_answer
    for sep in range(4):
        border = jnp.concatenate(pick(blocks(root_answer), sep_index_ref[sep]), axis=1)
        joined = split2(jnp.concatenate([solved[sep], border], axis=1))
        answer = stacked_products(dot_nn, joined, (high_ref[sep], low_ref[sep]))
        sep_out_ref[sep] = answer
        full[sep, :, :512] = answer
        full[sep, :, 512:] = border

    def gather(leaf, _):
        picked = pick(blocks(full[parent_ref[leaf]]), index_ref[leaf])
        down_ref[leaf] = jnp.concatenate(picked, axis=1)
        return 0

    lax.fori_loop(0, 16, gather, 0)


def upper_solve(place, parent, updates, index, sep_rhs, sep_slots, sep_index, root_rhs, own, other):
    return pl.pallas_call(
        upper_kernel,
        out_shape=(
            jax.ShapeDtypeStruct((16, 16, 512), F32),
            jax.ShapeDtypeStruct((4, 16, 512), F32),
            jax.ShapeDtypeStruct((16, 512), F32),
        ),
        in_specs=[full_smem()] * 2 + [full_vmem()] * 6 + [anywhere()] * 2,
        out_specs=(full_vmem(),) * 3,
        scratch_shapes=[
            pltpu.VMEM((4, 16, 512), F32),
            pltpu.VMEM((4, 16, 1024), F32),
            pltpu.VMEM((4, NZ, NC, 32, 512), F32),
            pltpu.VMEM((NZ, NC, 16, 512), F32),
            pltpu.VMEM((4, 1024, 512), BF16),
            pltpu.VMEM((4, 1024, 512), BF16),
            pltpu.SemaphoreType.DMA((10,)),
        ],
        compiler_params=params(28),
        name="upper_solve",
    )(place, parent, updates, index, sep_rhs, sep_slots, sep_index, root_rhs, own, other)


def inverse_rows(index, extent):
    place = jnp.arange(index.shape[1], dtype=jnp.int32)[None, :, None]
    slot = jnp.arange(extent, dtype=jnp.int32)[None, None, :]
    return jnp.max(jnp.where(index[:, :, None] == slot, place, -1), axis=1)


def swap_cores(value):
    return lax.ppermute(value, "c", [(0, 1), (1, 0)])


def local(
    leaf_rhs,
    leaf_factor,
    pivot_count,
    parent,
    leaf_index,
    separator_rhs,
    separator_factor,
    separator_index,
    root_rhs,
    root_factor,
):
    place = lax.axis_index("c").astype(jnp.int32)[None]
    rhs = leaf_rhs[0]
    slots = inverse_rows(leaf_index, 1024)[:, None, :]
    sep_slots = inverse_rows(separator_index, 512)[:, None, :]
    sep_rhs = jnp.transpose(separator_rhs[0], (1, 0, 2))
    shard = jnp.concatenate(
        [leaf_factor[0, :, :512], leaf_factor[0, :, 512:], separator_factor.reshape(128, 512), root_factor],
        axis=0,
    )
    line = lax.all_gather(shard, "z", axis=0, tiled=False)
    line, slots, sep_slots, sep_rhs = lax.optimization_barrier((line, slots, sep_slots, sep_rhs))
    own_border = line[10:, :96]
    other_border = swap_cores(own_border)
    line, own_border, other_border = lax.optimization_barrier((line, own_border, other_border))
    other_line = swap_cores(line)

    border = leaf_border(place, pivot_count, rhs, own_border, other_border)
    incoming = lax.all_to_all(
        border.reshape(16, 16, 512), ("y", "x"), split_axis=0, concat_axis=0, tiled=True
    )
    part, high, low = leaf_pivot(place, pivot_count, rhs, line, other_line)
    updates = spread_updates(parent, incoming, slots)
    down, sep_answer, root_answer = upper_solve(
        place, parent, updates, leaf_index[:, None, :], sep_rhs, sep_slots,
        separator_index[:, None, :], root_rhs[0], line, other_line,
    )
    received = lax.all_to_all(down, ("y", "x"), split_axis=0, concat_axis=0, tiled=True)
    leaf_answer = leaf_last(pivot_count, part, received.reshape(256, 512), high, low)
    return leaf_answer[None], jnp.transpose(sep_answer, (1, 0, 2))[None], root_answer[None]


def solution(mesh):
    fine = Mesh(mesh.devices.reshape(NY, NX, NZ, NC), ("y", "x", "z", "c"))
    leaf, src = ("y", "x"), ("z", "c")
    return jax.shard_map(
        local,
        mesh=fine,
        in_specs=(
            P(leaf, src, None),
            P(leaf, src, None),
            P(leaf),
            P(),
            P(),
            P(leaf, src, None, None),
            P(None, src, None),
            P(),
            P(leaf, src, None),
            P(src, None),
        ),
        out_specs=(P(leaf, src, None), P(leaf, src, None, None), P(leaf, src, None)),
        check_vma=False,
    )
```

```python
import jax
import jax.numpy as jnp
from jax import lax
from jax.experimental import pallas as pl
from jax.experimental.pallas import tpu as pltpu
from jax.sharding import Mesh, PartitionSpec as P

NY, NX, NZ, NC = 4, 4, 16, 2
F32, BF16 = jnp.float32, jnp.bfloat16
LANES = 128


def split2(value):
    high = value.astype(BF16)
    return high, (value - high.astype(F32)).astype(BF16)


def dot_nt(a, b):
    return lax.dot_general(a, b, (((1,), (1,)), ((), ())), preferred_element_type=F32)


def dot_nn(a, b):
    return lax.dot_general(a, b, (((1,), (0,)), ((), ())), preferred_element_type=F32)


def three_products(dot, a, b):
    return dot(a[0], b[0]) + (dot(a[1], b[0]) + dot(a[0], b[1]))


def stacked_products(dot, a, b):
    rows = a[0].shape[0]
    both = dot(jnp.concatenate([a[0], a[1]], axis=0), b[0])
    return both[:rows] + (both[rows:] + dot(a[0], b[1]))


def params(mebibytes):
    return pltpu.CompilerParams(vmem_limit_bytes=mebibytes * 1024 * 1024)


def full_vmem():
    return pl.BlockSpec(memory_space=pltpu.VMEM)


def full_smem():
    return pl.BlockSpec(memory_space=pltpu.SMEM)


def in_hbm():
    return pl.BlockSpec(memory_space=pltpu.HBM)


def anywhere():
    return pl.BlockSpec(memory_space=pl.ANY)


def start_all(copies):
    for copy in copies:
        copy.start()


def wait_all(copies):
    for copy in copies:
        copy.wait()


LEAF_ROWS, SHARD = 48, 56


def join_kernel(leaf_ref, root_ref, out_ref):
    out_ref[:LEAF_ROWS] = leaf_ref[...]
    out_ref[LEAF_ROWS:, :512] = root_ref[:8]
    out_ref[LEAF_ROWS:, 512:] = root_ref[8:]


def join(leaf, root):
    return pl.pallas_call(
        join_kernel,
        out_shape=jax.ShapeDtypeStruct((SHARD, 1024), F32),
        in_specs=[full_vmem()] * 2,
        out_specs=full_vmem(),
        compiler_params=params(60),
        name="join",
    )(leaf, root)


def leaf_copy(line_ref, buffer, first, count, sem):
    return pltpu.make_async_copy(line_ref.at[pl.ds(first, count), pl.ds(0, LEAF_ROWS), :], buffer, sem)


def leaf_border_kernel(count_ref, rhs_hbm, line_ref, border_ref, rhs_ref, buffer, sem, rhs_sem):
    copy = leaf_copy(line_ref, buffer, 21, 11, sem)
    load = pltpu.make_async_copy(rhs_hbm, rhs_ref, rhs_sem)
    load.start()
    copy.start()
    load.wait()
    cols = lax.broadcasted_iota(jnp.int32, rhs_ref.shape, 1)
    rhs = split2(jnp.where(cols < count_ref[0], rhs_ref[...], 0.0))
    copy.wait()
    rows = buffer[...].reshape(528, 1024)
    for block in range(2):
        first = 16 + 256 * block
        border_ref[:, 256 * block : 256 * (block + 1)] = three_products(
            dot_nt, rhs, split2(rows[first : first + 256])
        )


def leaf_border(count, rhs, line):
    return pl.pallas_call(
        leaf_border_kernel,
        out_shape=jax.ShapeDtypeStruct((256, 512), F32),
        in_specs=[full_smem(), in_hbm(), in_hbm()],
        out_specs=full_vmem(),
        scratch_shapes=[
            pltpu.VMEM((256, 1024), F32),
            pltpu.VMEM((11, 48, 1024), F32),
            pltpu.SemaphoreType.DMA,
            pltpu.SemaphoreType.DMA,
        ],
        compiler_params=params(60),
        name="leaf_border",
    )(count, rhs, line)


def leaf_pivot_kernel(
    count_ref, rhs_hbm, line_ref,
    part_hbm, border_high_hbm, border_low_hbm,
    rhs_ref, buffer, border_buffer, high_ref, low_ref, part_ref, border_high_ref, border_low_ref, sem, out_sem,
):
    copy = leaf_copy(line_ref, buffer, 0, 22, sem.at[0])
    border_copy = leaf_copy(line_ref, border_buffer, 21, 11, sem.at[1])
    load = pltpu.make_async_copy(rhs_hbm, rhs_ref, sem.at[2])
    load.start()
    copy.start()
    border_copy.start()
    count = count_ref[0]
    load.wait()
    cols = lax.broadcasted_iota(jnp.int32, rhs_ref.shape, 1)
    rhs = split2(jnp.where(cols < count, rhs_ref[...], 0.0))
    copy.wait()
    top = buffer[...].reshape(1056, 1024)
    solved = []
    for block in range(4):
        first, wide = 256 * block, 256 * (block + 1)
        rows = first + lax.broadcasted_iota(jnp.int32, (256, wide), 0)
        columns = lax.broadcasted_iota(jnp.int32, (256, wide), 1)
        values = jnp.where(columns < rows, top[first:wide, :wide], 0.0)
        values = jnp.where(columns == rows, 1.0, values)
        values = jnp.where(rows < count, values, 0.0)
        high, low = split2(values)
        high_ref[first:wide, :wide] = high
        low_ref[first:wide, :wide] = low
        solved.append(three_products(dot_nt, (rhs[0][:, :wide], rhs[1][:, :wide]), (high, low)))
    solved = split2(jnp.concatenate(solved, axis=1))
    border_copy.wait()
    border = border_buffer[...].reshape(528, 1024)
    stores = []
    for block in range(4):
        first, wide = 256 * block, 256 * (block + 1)
        border_high_ref[block], border_low_ref[block] = split2(border[16:, first:wide])
        part_ref[block] = three_products(
            dot_nn,
            (solved[0][:, first:], solved[1][:, first:]),
            (high_ref[first:, first:wide], low_ref[first:, first:wide]),
        )
        stores += [
            pltpu.make_async_copy(part_ref.at[block], part_hbm.at[block], out_sem.at[block, 0]),
            pltpu.make_async_copy(border_high_ref.at[block], border_high_hbm.at[block], out_sem.at[block, 1]),
            pltpu.make_async_copy(border_low_ref.at[block], border_low_hbm.at[block], out_sem.at[block, 2]),
        ]
        start_all(stores[-3:])
    wait_all(stores)


def leaf_pivot(count, rhs, line):
    return pl.pallas_call(
        leaf_pivot_kernel,
        out_shape=(
            jax.ShapeDtypeStruct((4, 256, 256), F32),
            jax.ShapeDtypeStruct((4, 512, 256), BF16),
            jax.ShapeDtypeStruct((4, 512, 256), BF16),
        ),
        in_specs=[full_smem(), in_hbm(), in_hbm()],
        out_specs=(in_hbm(),) * 3,
        scratch_shapes=[
            pltpu.VMEM((256, 1024), F32),
            pltpu.VMEM((22, 48, 1024), F32),
            pltpu.VMEM((11, 48, 1024), F32),
            pltpu.VMEM((1024, 1024), BF16),
            pltpu.VMEM((1024, 1024), BF16),
            pltpu.VMEM((4, 256, 256), F32),
            pltpu.VMEM((4, 512, 256), BF16),
            pltpu.VMEM((4, 512, 256), BF16),
            pltpu.SemaphoreType.DMA((3,)),
            pltpu.SemaphoreType.DMA((4, 3)),
        ],
        compiler_params=params(60),
        name="leaf_pivot",
    )(count, rhs, line)


def leaf_last_kernel(
    count_ref, part_hbm, border_ref, high_hbm, low_hbm, out_hbm,
    part_ref, high_ref, low_ref, out_ref, sem, out_sem,
):
    copies = [
        [
            pltpu.make_async_copy(source.at[block], to.at[block], sem.at[block, at])
            for at, (source, to) in enumerate(((high_hbm, high_ref), (low_hbm, low_ref), (part_hbm, part_ref)))
        ]
        for block in range(4)
    ]
    for group in copies:
        start_all(group)
    border = split2(border_ref[...])
    stores = []
    for block in range(4):
        wait_all(copies[block])
        answer = part_ref[block] + three_products(dot_nn, border, (high_ref[block], low_ref[block]))
        cols = 256 * block + lax.broadcasted_iota(jnp.int32, answer.shape, 1)
        out_ref[block] = jnp.where(cols < count_ref[0], answer, 0.0)
        stores.append(
            pltpu.make_async_copy(out_ref.at[block], out_hbm.at[:, pl.ds(256 * block, 256)], out_sem.at[block])
        )
        stores[-1].start()
    wait_all(stores)


def leaf_last(count, part, border, high, low):
    return pl.pallas_call(
        leaf_last_kernel,
        out_shape=jax.ShapeDtypeStruct((256, 1024), F32),
        in_specs=[full_smem(), in_hbm(), full_vmem(), in_hbm(), in_hbm()],
        out_specs=in_hbm(),
        scratch_shapes=[
            pltpu.VMEM((4, 256, 256), F32),
            pltpu.VMEM((4, 512, 256), BF16),
            pltpu.VMEM((4, 512, 256), BF16),
            pltpu.VMEM((4, 256, 256), F32),
            pltpu.SemaphoreType.DMA((4, 3)),
            pltpu.SemaphoreType.DMA((4,)),
        ],
        compiler_params=params(60),
        name="leaf_last",
    )(count, part, border, high, low)


def pick(values, index_row):
    out = []
    for block in range(index_row.shape[1] // LANES):
        index = jnp.broadcast_to(index_row[:, block * LANES : (block + 1) * LANES], (16, LANES))
        lane, source = index & (LANES - 1), index >> 7
        total = jnp.zeros((16, LANES), F32)
        for at, value in enumerate(values):
            taken = jnp.take_along_axis(value, lane, axis=1)
            total = jnp.where(source == at, taken, total)
        out.append(total)
    return out


def blocks(value):
    return [value[:, at * LANES : (at + 1) * LANES] for at in range(value.shape[1] // LANES)]


OFFSETS = (0, -1, 1, -2)


def upper_operator_kernel(place_ref, *refs):
    own_refs, other_refs, line_ref = refs[:5], refs[5:10], refs[10]
    high_hbm, low_hbm, root_high_hbm, root_low_hbm = refs[11:15]
    buffer, root_buffer, high_ref, low_ref, root_high_ref, root_low_ref, sem, root_sem, out_sem = refs[15:]
    y, x, c = place_ref[0], place_ref[1], place_ref[2]
    for piece_refs, parity in ((own_refs, c), (other_refs, 1 - c)):
        for outer in range(4):
            for inner in range(4):
                if outer < 3:
                    source = piece_refs[outer].at[inner]
                else:
                    source = piece_refs[3 + inner // 2].at[inner % 2]
                along_y = jnp.where(parity == 0, OFFSETS[outer], OFFSETS[inner])
                along_x = jnp.where(parity == 0, OFFSETS[inner], OFFSETS[outer])
                group = jnp.where(parity == 0, outer, inner)
                to_y = lax.rem(y + along_y + 8, 4)
                to_x = lax.rem(x + along_x + 8, 4)
                pltpu.make_async_copy(source, buffer.at[to_y, to_x, parity], sem.at[group]).start()
    root_copies = [
        pltpu.make_async_copy(
            line_ref.at[:, pl.ds(LEAF_ROWS, 8), pl.ds(512 * half, 512)],
            root_buffer.at[:, pl.ds(8 * half, 8), :],
            root_sem.at[half],
        )
        for half in range(2)
    ]
    start_all(root_copies)
    stores = []

    def send(value_ref, to_ref, at):
        stores.append(pltpu.make_async_copy(value_ref, to_ref, out_sem.at[at]))
        stores[-1].start()

    for group in range(4):
        for _ in range(8):
            pltpu.make_async_copy(own_refs[0].at[0], buffer.at[0, 0, 0], sem.at[group]).wait()
        sep = lax.rem(y + OFFSETS[group] + 8, 4)

        def rows(z, parity):
            return jnp.concatenate([buffer[sep, q, parity, z] for q in range(4)], axis=0)

        def pivot_rows(z, _):
            for parity in range(2):
                shard = 2 * z + parity
                row_ids = shard * 32 + lax.broadcasted_iota(jnp.int32, (32, 512), 0)
                col_ids = lax.broadcasted_iota(jnp.int32, (32, 512), 1)
                value = lower_unit(rows(z, parity), row_ids, col_ids)
                to = pl.ds(pl.multiple_of(shard * 32, 32), 32)
                high_ref[sep, to], low_ref[sep, to] = split2(value)
            return 0

        def border_rows(z, _):
            for parity in range(2):
                to = pl.ds(pl.multiple_of((2 * z + parity) * 32, 32), 32)
                high_ref[sep, to], low_ref[sep, to] = split2(rows(z, parity))
            return 0

        lax.fori_loop(0, 8, pivot_rows, 0)
        lax.fori_loop(8, 16, border_rows, 0)
        send(high_ref.at[sep], high_hbm.at[sep], 2 * group)
        send(low_ref.at[sep], low_hbm.at[sep], 2 * group + 1)
    wait_all(root_copies)
    row_ids = lax.broadcasted_iota(jnp.int32, (512, 512), 0)
    col_ids = lax.broadcasted_iota(jnp.int32, (512, 512), 1)
    value = lower_unit(root_buffer[...].reshape(512, 512), row_ids, col_ids)
    root_high_ref[...], root_low_ref[...] = split2(value)
    send(root_high_ref, root_high_hbm, 8)
    send(root_low_ref, root_low_hbm, 9)
    wait_all(stores)


def lower_unit(value, row_ids, col_ids):
    return jnp.where(col_ids == row_ids, 1.0, jnp.where(col_ids < row_ids, value, 0.0))


def upper_operators(place, own, other, line):
    return pl.pallas_call(
        upper_operator_kernel,
        out_shape=(
            jax.ShapeDtypeStruct((4, 1024, 512), BF16),
            jax.ShapeDtypeStruct((4, 1024, 512), BF16),
            jax.ShapeDtypeStruct((512, 512), BF16),
            jax.ShapeDtypeStruct((512, 512), BF16),
        ),
        in_specs=[full_smem()] + [in_hbm()] * 11,
        out_specs=(in_hbm(),) * 4,
        scratch_shapes=[
            pltpu.VMEM((NY, NX, NC, NZ, 8, 512), F32),
            pltpu.VMEM((32, 16, 512), F32),
            pltpu.VMEM((4, 1024, 512), BF16),
            pltpu.VMEM((4, 1024, 512), BF16),
            pltpu.VMEM((512, 512), BF16),
            pltpu.VMEM((512, 512), BF16),
            pltpu.SemaphoreType.DMA((4,)),
            pltpu.SemaphoreType.DMA((2,)),
            pltpu.SemaphoreType.DMA((10,)),
        ],
        compiler_params=params(60),
        name="upper_operators",
    )(place, *own, *other, line)


def upper_kernel(
    parent_ref, incoming_ref, slot_ref, index_ref, sep_rhs_ref, sep_slot_ref, sep_index_ref, root_rhs_ref,
    high_hbm, low_hbm, root_high_hbm, root_low_hbm,
    down_ref, sep_out_ref, root_out_ref,
    updates, solved, full, high_ref, low_ref, root_high_ref, root_low_ref, sem,
):
    loads = []
    for sep in range(4):
        loads.append([
            pltpu.make_async_copy(high_hbm.at[sep], high_ref.at[sep], sem.at[sep, 0]),
            pltpu.make_async_copy(low_hbm.at[sep], low_ref.at[sep], sem.at[sep, 1]),
        ])
    loads.append([
        pltpu.make_async_copy(root_high_hbm, root_high_ref, sem.at[4, 0]),
        pltpu.make_async_copy(root_low_hbm, root_low_ref, sem.at[4, 1]),
    ])
    for group in loads:
        start_all(group)
    updates[...] = jnp.zeros(updates.shape, F32)

    def spread(leaf, _):
        to = parent_ref[leaf]
        picked = pick(blocks(incoming_ref[leaf]), slot_ref[leaf])
        for at, value in enumerate(picked):
            part = slice(at * LANES, (at + 1) * LANES)
            updates[to, :, part] = updates[to, :, part] + value
        return 0

    lax.fori_loop(0, 16, spread, 0, unroll=4)
    root_total = root_rhs_ref[...]
    for sep in range(4):
        wait_all(loads[sep])
        pivot = split2(sep_rhs_ref[sep] + updates[sep, :, :512])
        forward = stacked_products(dot_nt, pivot, (high_ref[sep], low_ref[sep]))
        solved[sep] = forward[:, :512]
        border = forward[:, 512:] + updates[sep, :, 512:]
        root_total = root_total + jnp.concatenate(pick(blocks(border), sep_slot_ref[sep]), axis=1)
    wait_all(loads[4])
    root = (root_high_ref[...], root_low_ref[...])
    root_solved = stacked_products(dot_nt, split2(root_total), root)
    root_answer = stacked_products(dot_nn, split2(root_solved), root)
    root_out_ref[...] = root_answer
    for sep in range(4):
        border = jnp.concatenate(pick(blocks(root_answer), sep_index_ref[sep]), axis=1)
        joined = split2(jnp.concatenate([solved[sep], border], axis=1))
        answer = stacked_products(dot_nn, joined, (high_ref[sep], low_ref[sep]))
        sep_out_ref[sep] = answer
        full[sep, :, :512] = answer
        full[sep, :, 512:] = border

    def gather(leaf, _):
        picked = pick(blocks(full[parent_ref[leaf]]), index_ref[leaf])
        down_ref[leaf] = jnp.concatenate(picked, axis=1)
        return 0

    lax.fori_loop(0, 16, gather, 0, unroll=4)


def upper_solve(parent, incoming, slots, index, sep_rhs, sep_slots, sep_index, root_rhs, operators):
    return pl.pallas_call(
        upper_kernel,
        out_shape=(
            jax.ShapeDtypeStruct((16, 16, 512), F32),
            jax.ShapeDtypeStruct((4, 16, 512), F32),
            jax.ShapeDtypeStruct((16, 512), F32),
        ),
        in_specs=[full_smem()] + [full_vmem()] * 7 + [in_hbm()] * 4,
        out_specs=(full_vmem(),) * 3,
        scratch_shapes=[
            pltpu.VMEM((4, 16, 1024), F32),
            pltpu.VMEM((4, 16, 512), F32),
            pltpu.VMEM((4, 16, 1024), F32),
            pltpu.VMEM((4, 1024, 512), BF16),
            pltpu.VMEM((4, 1024, 512), BF16),
            pltpu.VMEM((512, 512), BF16),
            pltpu.VMEM((512, 512), BF16),
            pltpu.SemaphoreType.DMA((5, 2)),
        ],
        compiler_params=params(60),
        name="upper_solve",
    )(parent, incoming, slots, index, sep_rhs, sep_slots, sep_index, root_rhs, *operators)


def inverse_rows(index, extent):
    place = jnp.arange(index.shape[1], dtype=jnp.int32)[None, :, None]
    slot = jnp.arange(extent, dtype=jnp.int32)[None, None, :]
    return jnp.max(jnp.where(index[:, :, None] == slot, place, -1), axis=1)


def swap_cores(value):
    return lax.ppermute(value, "c", [(0, 1), (1, 0)])


def along_plane(value, step, first):
    pairs = []
    for y in range(NY):
        for x in range(NX):
            for c in range(NC):
                by_x = (c == 0) == first
                to_y, to_x = (y, (x + step) % NX) if by_x else ((y + step) % NY, x)
                pairs.append(((y * NX + x) * NC + c, (to_y * NX + to_x) * NC + c))
    return lax.ppermute(value, ("y", "x", "c"), pairs)


def gather_plane(value, first, beside):
    ahead = along_plane(value, 1, first)
    back = along_plane(value, -1, first)
    ahead, back, beside = lax.optimization_barrier((ahead, back, beside))
    half = value.shape[0] // 2
    far_low = along_plane(ahead[:half], 1, first)
    far_high = along_plane(back[half:], -1, first)
    return (value, ahead, back, far_low, far_high), beside


def gather_line(separator_factor, y, x):
    mine = lax.dynamic_slice(separator_factor, (y, 8 * x, 0), (1, 8, 512))
    return lax.all_to_all(
        jnp.broadcast_to(mine, (NZ, 8, 512)), "z", split_axis=0, concat_axis=0, tiled=True
    )


def spread_line(line, beside):
    rows = jnp.stack([line, along_plane(line, 1, True), along_plane(line, -1, True), along_plane(line, 2, True)])
    return gather_plane(rows, False, beside)


def local(
    leaf_rhs,
    leaf_factor,
    pivot_count,
    parent,
    leaf_index,
    separator_rhs,
    separator_factor,
    separator_index,
    root_rhs,
    root_factor,
):
    rhs = leaf_rhs[0]
    slots = inverse_rows(leaf_index, 1024)[:, None, :]
    sep_slots = inverse_rows(separator_index, 512)[:, None, :]
    sep_rhs = jnp.transpose(separator_rhs[0], (1, 0, 2))
    y, x, c = lax.axis_index("y"), lax.axis_index("x"), lax.axis_index("c")
    place = jnp.stack([y, x, c]).astype(jnp.int32)
    line = lax.all_gather(join(leaf_factor[0], root_factor), ("z", "c"), axis=0, tiled=False)
    sep_line = gather_line(separator_factor, y, x)
    (rows, ahead, back, far_low, far_high), slots = spread_line(sep_line, slots)
    near_swapped = (swap_cores(rows), swap_cores(ahead), swap_cores(back))

    line, sep_slots, sep_rhs = lax.optimization_barrier((line, sep_slots, sep_rhs))
    border = leaf_border(pivot_count, rhs, line)
    far_low, far_high, line, border = lax.optimization_barrier((far_low, far_high, line, border))
    own_set = (rows, ahead, back, far_low, far_high)
    other_set = near_swapped + (swap_cores(far_low), swap_cores(far_high))
    incoming = lax.all_to_all(
        border.reshape(16, 16, 512), ("y", "x"), split_axis=0, concat_axis=0, tiled=True
    )
    operators = upper_operators(place, own_set, other_set, line)
    down, sep_answer, root_answer = upper_solve(
        parent, incoming, slots, leaf_index[:, None, :], sep_rhs, sep_slots,
        separator_index[:, None, :], root_rhs[0], operators,
    )
    line, down = lax.optimization_barrier((line, down))
    received = lax.all_to_all(down, ("y", "x"), split_axis=0, concat_axis=0, tiled=True)
    part, high, low = leaf_pivot(pivot_count, rhs, line)
    leaf_answer = leaf_last(pivot_count, part, received.reshape(256, 512), high, low)
    return leaf_answer[None], jnp.transpose(sep_answer, (1, 0, 2))[None], root_answer[None]


def solution(mesh):
    fine = Mesh(mesh.devices.reshape(NY, NX, NZ, NC), ("y", "x", "z", "c"))
    leaf, src = ("y", "x"), ("z", "c")
    return jax.shard_map(
        local,
        mesh=fine,
        in_specs=(
            P(leaf, src, None),
            P(leaf, src, None),
            P(leaf),
            P(),
            P(),
            P(leaf, src, None, None),
            P(None, src, None),
            P(),
            P(leaf, src, None),
            P(src, None),
        ),
        out_specs=(P(leaf, src, None), P(leaf, src, None, None), P(leaf, src, None)),
        check_vma=False,
    )
```

```python
import jax
import jax.numpy as jnp
from jax import lax
from jax.experimental import pallas as pl
from jax.experimental.pallas import tpu as pltpu
from jax.sharding import Mesh, PartitionSpec as P

NY, NX, NZ, NC = 4, 4, 16, 2
F32, BF16 = jnp.float32, jnp.bfloat16
LANES = 128


def split2(value):
    high = value.astype(BF16)
    return high, (value - high.astype(F32)).astype(BF16)


def dot_nt(a, b):
    return lax.dot_general(a, b, (((1,), (1,)), ((), ())), preferred_element_type=F32)


def dot_nn(a, b):
    return lax.dot_general(a, b, (((1,), (0,)), ((), ())), preferred_element_type=F32)


def stack2(pair):
    return jnp.concatenate(pair, axis=0)


def stacked_products(dot, both, b):
    rows = both.shape[0] // 2
    first = dot(both, b[0])
    return first[:rows] + (first[rows:] + dot(both[:rows], b[1]))


def params(mebibytes):
    return pltpu.CompilerParams(vmem_limit_bytes=mebibytes * 1024 * 1024)


def full_vmem():
    return pl.BlockSpec(memory_space=pltpu.VMEM)


def full_smem():
    return pl.BlockSpec(memory_space=pltpu.SMEM)


def in_hbm():
    return pl.BlockSpec(memory_space=pltpu.HBM)


def anywhere():
    return pl.BlockSpec(memory_space=pl.ANY)


def start_all(copies):
    for copy in copies:
        copy.start()


def wait_all(copies):
    for copy in copies:
        copy.wait()


LEAF_ROWS, SHARD = 48, 56


def join_kernel(leaf_ref, root_ref, out_ref):
    out_ref[:LEAF_ROWS] = leaf_ref[...]
    out_ref[LEAF_ROWS:, :512] = root_ref[:8]
    out_ref[LEAF_ROWS:, 512:] = root_ref[8:]


def join(leaf, root):
    return pl.pallas_call(
        join_kernel,
        out_shape=jax.ShapeDtypeStruct((SHARD, 1024), F32),
        in_specs=[full_vmem()] * 2,
        out_specs=full_vmem(),
        compiler_params=params(60),
        name="join",
    )(leaf, root)


def leaf_copy(line_ref, buffer, first, count, sem):
    return pltpu.make_async_copy(line_ref.at[pl.ds(first, count), pl.ds(0, LEAF_ROWS), :], buffer, sem)


def leaf_border_kernel(count_ref, rhs_hbm, line_ref, border_ref, rhs_ref, buffer, sem, rhs_sem):
    copy = leaf_copy(line_ref, buffer, 21, 11, sem)
    load = pltpu.make_async_copy(rhs_hbm, rhs_ref, rhs_sem)
    load.start()
    copy.start()
    load.wait()
    cols = lax.broadcasted_iota(jnp.int32, rhs_ref.shape, 1)
    rhs = stack2(split2(jnp.where(cols < count_ref[0], rhs_ref[...], 0.0)))
    copy.wait()
    rows = buffer[...].reshape(528, 1024)
    for block in range(2):
        first = 16 + 256 * block
        border_ref[:, 256 * block : 256 * (block + 1)] = stacked_products(
            dot_nt, rhs, split2(rows[first : first + 256])
        )


def leaf_border(count, rhs, line):
    return pl.pallas_call(
        leaf_border_kernel,
        out_shape=jax.ShapeDtypeStruct((256, 512), F32),
        in_specs=[full_smem(), in_hbm(), in_hbm()],
        out_specs=full_vmem(),
        scratch_shapes=[
            pltpu.VMEM((256, 1024), F32),
            pltpu.VMEM((11, 48, 1024), F32),
            pltpu.SemaphoreType.DMA,
            pltpu.SemaphoreType.DMA,
        ],
        compiler_params=params(60),
        name="leaf_border",
    )(count, rhs, line)


def leaf_pivot_kernel(
    count_ref, rhs_hbm, line_ref,
    part_hbm, border_high_hbm, border_low_hbm,
    rhs_ref, buffer, border_buffer, high_ref, low_ref, part_ref, border_high_ref, border_low_ref, sem, out_sem,
):
    copy = leaf_copy(line_ref, buffer, 0, 22, sem.at[0])
    border_copy = leaf_copy(line_ref, border_buffer, 21, 11, sem.at[1])
    load = pltpu.make_async_copy(rhs_hbm, rhs_ref, sem.at[2])
    load.start()
    copy.start()
    border_copy.start()
    count = count_ref[0]
    load.wait()
    cols = lax.broadcasted_iota(jnp.int32, rhs_ref.shape, 1)
    rhs = stack2(split2(jnp.where(cols < count, rhs_ref[...], 0.0)))
    copy.wait()
    top = buffer[...].reshape(1056, 1024)
    solved = []
    for block in range(4):
        first, wide = 256 * block, 256 * (block + 1)
        rows = first + lax.broadcasted_iota(jnp.int32, (256, wide), 0)
        columns = lax.broadcasted_iota(jnp.int32, (256, wide), 1)
        values = jnp.where(columns < rows, top[first:wide, :wide], 0.0)
        values = jnp.where(columns == rows, 1.0, values)
        values = jnp.where(rows < count, values, 0.0)
        high, low = split2(values)
        high_ref[first:wide, :wide] = high
        low_ref[first:wide, :wide] = low
        solved.append(stacked_products(dot_nt, rhs[:, :wide], (high, low)))
    solved = stack2(split2(jnp.concatenate(solved, axis=1)))
    border_copy.wait()
    border = border_buffer[...].reshape(528, 1024)
    stores = []
    for block in range(4):
        first, wide = 256 * block, 256 * (block + 1)
        border_high_ref[block], border_low_ref[block] = split2(border[16:, first:wide])
        part_ref[block] = stacked_products(
            dot_nn,
            solved[:, first:],
            (high_ref[first:, first:wide], low_ref[first:, first:wide]),
        )
        stores += [
            pltpu.make_async_copy(part_ref.at[block], part_hbm.at[block], out_sem.at[block, 0]),
            pltpu.make_async_copy(border_high_ref.at[block], border_high_hbm.at[block], out_sem.at[block, 1]),
            pltpu.make_async_copy(border_low_ref.at[block], border_low_hbm.at[block], out_sem.at[block, 2]),
        ]
        start_all(stores[-3:])
    wait_all(stores)


def leaf_pivot(count, rhs, line):
    return pl.pallas_call(
        leaf_pivot_kernel,
        out_shape=(
            jax.ShapeDtypeStruct((4, 256, 256), F32),
            jax.ShapeDtypeStruct((4, 512, 256), BF16),
            jax.ShapeDtypeStruct((4, 512, 256), BF16),
        ),
        in_specs=[full_smem(), in_hbm(), in_hbm()],
        out_specs=(in_hbm(),) * 3,
        scratch_shapes=[
            pltpu.VMEM((256, 1024), F32),
            pltpu.VMEM((22, 48, 1024), F32),
            pltpu.VMEM((11, 48, 1024), F32),
            pltpu.VMEM((1024, 1024), BF16),
            pltpu.VMEM((1024, 1024), BF16),
            pltpu.VMEM((4, 256, 256), F32),
            pltpu.VMEM((4, 512, 256), BF16),
            pltpu.VMEM((4, 512, 256), BF16),
            pltpu.SemaphoreType.DMA((3,)),
            pltpu.SemaphoreType.DMA((4, 3)),
        ],
        compiler_params=params(60),
        name="leaf_pivot",
    )(count, rhs, line)


def leaf_last_kernel(
    count_ref, part_hbm, border_ref, high_hbm, low_hbm, out_hbm,
    part_ref, high_ref, low_ref, out_ref, sem, out_sem,
):
    copies = [
        [
            pltpu.make_async_copy(source.at[block], to.at[block], sem.at[block, at])
            for at, (source, to) in enumerate(((high_hbm, high_ref), (low_hbm, low_ref), (part_hbm, part_ref)))
        ]
        for block in range(4)
    ]
    for group in copies:
        start_all(group)
    border = stack2(split2(border_ref[...]))
    stores = []
    for block in range(4):
        wait_all(copies[block])
        answer = part_ref[block] + stacked_products(dot_nn, border, (high_ref[block], low_ref[block]))
        cols = 256 * block + lax.broadcasted_iota(jnp.int32, answer.shape, 1)
        out_ref[block] = jnp.where(cols < count_ref[0], answer, 0.0)
        stores.append(
            pltpu.make_async_copy(out_ref.at[block], out_hbm.at[:, pl.ds(256 * block, 256)], out_sem.at[block])
        )
        stores[-1].start()
    wait_all(stores)


def leaf_last(count, part, border, high, low):
    return pl.pallas_call(
        leaf_last_kernel,
        out_shape=jax.ShapeDtypeStruct((256, 1024), F32),
        in_specs=[full_smem(), in_hbm(), full_vmem(), in_hbm(), in_hbm()],
        out_specs=in_hbm(),
        scratch_shapes=[
            pltpu.VMEM((4, 256, 256), F32),
            pltpu.VMEM((4, 512, 256), BF16),
            pltpu.VMEM((4, 512, 256), BF16),
            pltpu.VMEM((4, 256, 256), F32),
            pltpu.SemaphoreType.DMA((4, 3)),
            pltpu.SemaphoreType.DMA((4,)),
        ],
        compiler_params=params(59),
        name="leaf_last",
    )(count, part, border, high, low)


LANE_GATHER = lax.GatherDimensionNumbers(
    offset_dims=(),
    collapsed_slice_dims=(1,),
    start_index_map=(1,),
    operand_batching_dims=(0,),
    start_indices_batching_dims=(0,),
)


def take_lanes(value, lane):
    return lax.gather(
        value, lane[..., None], LANE_GATHER, slice_sizes=(1, 1), mode=lax.GatherScatterMode.PROMISE_IN_BOUNDS
    )


def pick(values, index_row):
    out = []
    for block in range(index_row.shape[1] // LANES):
        index = jnp.broadcast_to(index_row[:, block * LANES : (block + 1) * LANES], (8, LANES))
        lane, found = index & (LANES - 1), index >= 0
        bits = [(index & (LANES << bit)) != 0 for bit in range(len(values).bit_length() - 1)]
        halves = []
        for half in range(2):
            level = [take_lanes(value[8 * half : 8 * half + 8], lane) for value in values]
            for bit in bits:
                level = [jnp.where(bit, odd, even) for even, odd in zip(level[::2], level[1::2])]
            halves.append(jnp.where(found, level[0], 0.0))
        out.append(jnp.concatenate(halves, axis=0))
    return out


def blocks(value):
    return [value[:, at * LANES : (at + 1) * LANES] for at in range(value.shape[1] // LANES)]


OFFSETS = (0, -1, 1, -2)
TILES = [min(4, z // 2 + 1) for z in range(NZ)]
FIRST_TILE = [sum(TILES[:z]) for z in range(NZ)]
PACKED = sum(TILES)


def pack_kernel(line_ref, out_ref):
    for z in range(NZ):
        for tile in range(TILES[z]):
            out_ref[FIRST_TILE[z] + tile] = line_ref[z, :, tile * LANES : (tile + 1) * LANES]


def pack(line):
    return pl.pallas_call(
        pack_kernel,
        out_shape=jax.ShapeDtypeStruct((PACKED, 8, LANES), F32),
        in_specs=[full_vmem()],
        out_specs=full_vmem(),
        compiler_params=params(60),
        name="pack",
    )(line)


def upper_operator_kernel(place_ref, *refs):
    own_refs, other_refs, line_ref = refs[:4], refs[4:8], refs[8]
    high_hbm, low_hbm, root_high_hbm, root_low_hbm = refs[9:13]
    buffer, root_buffer, high_ref, low_ref, root_high_ref, root_low_ref, sem, root_sem, out_sem = refs[13:]
    y, x, c = place_ref[0], place_ref[1], place_ref[2]
    for piece_refs, parity in ((own_refs, c), (other_refs, 1 - c)):
        for outer in range(4):
            for inner in range(4):
                source = piece_refs[outer].at[inner]
                along_y = jnp.where(parity == 0, OFFSETS[outer], OFFSETS[inner])
                along_x = jnp.where(parity == 0, OFFSETS[inner], OFFSETS[outer])
                group = jnp.where(parity == 0, outer, inner)
                to_y = lax.rem(y + along_y + 8, 4)
                to_x = lax.rem(x + along_x + 8, 4)
                pltpu.make_async_copy(source, buffer.at[to_y, to_x, parity], sem.at[group]).start()
    root_copies = [
        pltpu.make_async_copy(
            line_ref.at[:, pl.ds(LEAF_ROWS, 8), pl.ds(512 * half, 512)],
            root_buffer.at[:, pl.ds(8 * half, 8), :],
            root_sem.at[half],
        )
        for half in range(2)
    ]
    start_all(root_copies)

    def out_copies(group):
        offset = jnp.int32(OFFSETS[0])
        for at in range(1, 4):
            offset = jnp.where(group == at, OFFSETS[at], offset)
        sep = lax.rem(y + offset + 8, 4)
        return sep, [
            pltpu.make_async_copy(high_ref.at[sep], high_hbm.at[sep], out_sem.at[2 * group]),
            pltpu.make_async_copy(low_ref.at[sep], low_hbm.at[sep], out_sem.at[2 * group + 1]),
        ]

    def one_group(group, _):
        for _ in range(8):
            pltpu.make_async_copy(own_refs[0].at[0], buffer.at[0, 0, 0], sem.at[group]).wait()
        sep, copies = out_copies(group)

        def rows(parity, first, tiles):
            return jnp.concatenate([
                jnp.concatenate([buffer[sep, q, parity, first + tile] for tile in range(tiles)], axis=1)
                for q in range(4)
            ], axis=0)

        for z in range(8):
            width = TILES[z] * LANES
            for parity in range(2):
                first_row = 32 * (2 * z + parity)
                row_ids = first_row + lax.broadcasted_iota(jnp.int32, (32, width), 0)
                col_ids = lax.broadcasted_iota(jnp.int32, (32, width), 1)
                value = lower_unit(rows(parity, FIRST_TILE[z], TILES[z]), row_ids, col_ids)
                high, low = split2(value)
                to = slice(first_row, first_row + 32)
                high_ref[sep, to, :width] = high
                low_ref[sep, to, :width] = low
                if width < 512:
                    high_ref[sep, to, width:] = jnp.zeros((32, 512 - width), BF16)
                    low_ref[sep, to, width:] = jnp.zeros((32, 512 - width), BF16)

        def border_rows(z, _):
            for parity in range(2):
                to = pl.ds(pl.multiple_of((2 * z + parity) * 32, 32), 32)
                high_ref[sep, to], low_ref[sep, to] = split2(rows(parity, FIRST_TILE[8] + 4 * (z - 8), 4))
            return 0

        lax.fori_loop(8, 16, border_rows, 0)
        start_all(copies)
        return 0

    lax.fori_loop(0, 4, one_group, 0)
    wait_all(root_copies)
    row_ids = lax.broadcasted_iota(jnp.int32, (512, 512), 0)
    col_ids = lax.broadcasted_iota(jnp.int32, (512, 512), 1)
    value = lower_unit(root_buffer[...].reshape(512, 512), row_ids, col_ids)
    root_high_ref[...], root_low_ref[...] = split2(value)
    root_stores = [
        pltpu.make_async_copy(root_high_ref, root_high_hbm, out_sem.at[8]),
        pltpu.make_async_copy(root_low_ref, root_low_hbm, out_sem.at[9]),
    ]
    start_all(root_stores)
    for group in range(4):
        wait_all(out_copies(group)[1])
    wait_all(root_stores)


def lower_unit(value, row_ids, col_ids):
    return jnp.where(col_ids == row_ids, 1.0, jnp.where(col_ids < row_ids, value, 0.0))


def upper_operators(place, own, other, line):
    return pl.pallas_call(
        upper_operator_kernel,
        out_shape=(
            jax.ShapeDtypeStruct((4, 1024, 512), BF16),
            jax.ShapeDtypeStruct((4, 1024, 512), BF16),
            jax.ShapeDtypeStruct((512, 512), BF16),
            jax.ShapeDtypeStruct((512, 512), BF16),
        ),
        in_specs=[full_smem()] + [in_hbm()] * 9,
        out_specs=(in_hbm(),) * 4,
        scratch_shapes=[
            pltpu.VMEM((NY, NX, NC, PACKED, 8, LANES), F32),
            pltpu.VMEM((32, 16, 512), F32),
            pltpu.VMEM((4, 1024, 512), BF16),
            pltpu.VMEM((4, 1024, 512), BF16),
            pltpu.VMEM((512, 512), BF16),
            pltpu.VMEM((512, 512), BF16),
            pltpu.SemaphoreType.DMA((4,)),
            pltpu.SemaphoreType.DMA((2,)),
            pltpu.SemaphoreType.DMA((10,)),
        ],
        compiler_params=params(60),
        name="upper_operators",
    )(place, *own, *other, line)


def upper_kernel(
    parent_ref, incoming_ref, slot_ref, index_ref, sep_rhs_ref, sep_slot_ref, sep_index_ref, root_rhs_ref,
    high_hbm, low_hbm, root_high_hbm, root_low_hbm,
    down_ref, sep_out_ref, root_out_ref,
    updates, solved, full, high_ref, low_ref, root_high_ref, root_low_ref, sem,
):
    loads = []
    for sep in range(4):
        loads.append([
            pltpu.make_async_copy(high_hbm.at[sep], high_ref.at[sep], sem.at[sep, 0]),
            pltpu.make_async_copy(low_hbm.at[sep], low_ref.at[sep], sem.at[sep, 1]),
        ])
    loads.append([
        pltpu.make_async_copy(root_high_hbm, root_high_ref, sem.at[4, 0]),
        pltpu.make_async_copy(root_low_hbm, root_low_ref, sem.at[4, 1]),
    ])
    for group in loads:
        start_all(group)
    updates[...] = jnp.zeros(updates.shape, F32)

    def spread(leaf, _):
        to = parent_ref[leaf]
        picked = pick(blocks(incoming_ref[leaf]), slot_ref[leaf])
        for at, value in enumerate(picked):
            part = slice(at * LANES, (at + 1) * LANES)
            updates[to, :, part] = updates[to, :, part] + value
        return 0

    lax.fori_loop(0, 16, spread, 0, unroll=4)
    root_total = root_rhs_ref[...]
    for sep in range(4):
        wait_all(loads[sep])
        pivot = stack2(split2(sep_rhs_ref[sep] + updates[sep, :, :512]))
        solved[sep, :, :256] = stacked_products(
            dot_nt, pivot[:, :256], (high_ref[sep, :256, :256], low_ref[sep, :256, :256])
        )
        forward = stacked_products(dot_nt, pivot, (high_ref[sep, 256:], low_ref[sep, 256:]))
        solved[sep, :, 256:] = forward[:, :256]
        border = forward[:, 256:] + updates[sep, :, 512:]
        root_total = root_total + jnp.concatenate(pick(blocks(border), sep_slot_ref[sep]), axis=1)
    wait_all(loads[4])
    root = (root_high_ref[...], root_low_ref[...])
    root_solved = stacked_products(dot_nt, stack2(split2(root_total)), root)
    root_answer = stacked_products(dot_nn, stack2(split2(root_solved)), root)
    root_out_ref[...] = root_answer
    for sep in range(4):
        border = jnp.concatenate(pick(blocks(root_answer), sep_index_ref[sep]), axis=1)
        joined = stack2(split2(jnp.concatenate([solved[sep], border], axis=1)))
        left = stacked_products(dot_nn, joined, (high_ref[sep, :, :256], low_ref[sep, :, :256]))
        right = stacked_products(dot_nn, joined[:, 256:], (high_ref[sep, 256:, 256:], low_ref[sep, 256:, 256:]))
        sep_out_ref[sep, :, :256] = left
        sep_out_ref[sep, :, 256:] = right
        full[sep, :, :256] = left
        full[sep, :, 256:512] = right
        full[sep, :, 512:] = border

    def gather(leaf, _):
        picked = pick(blocks(full[parent_ref[leaf]]), index_ref[leaf])
        down_ref[leaf] = jnp.concatenate(picked, axis=1)
        return 0

    lax.fori_loop(0, 16, gather, 0, unroll=4)


def upper_solve(parent, incoming, slots, index, sep_rhs, sep_slots, sep_index, root_rhs, operators):
    return pl.pallas_call(
        upper_kernel,
        out_shape=(
            jax.ShapeDtypeStruct((16, 16, 512), F32),
            jax.ShapeDtypeStruct((4, 16, 512), F32),
            jax.ShapeDtypeStruct((16, 512), F32),
        ),
        in_specs=[full_smem()] + [full_vmem()] * 7 + [in_hbm()] * 4,
        out_specs=(full_vmem(),) * 3,
        scratch_shapes=[
            pltpu.VMEM((4, 16, 1024), F32),
            pltpu.VMEM((4, 16, 512), F32),
            pltpu.VMEM((4, 16, 1024), F32),
            pltpu.VMEM((4, 1024, 512), BF16),
            pltpu.VMEM((4, 1024, 512), BF16),
            pltpu.VMEM((512, 512), BF16),
            pltpu.VMEM((512, 512), BF16),
            pltpu.SemaphoreType.DMA((5, 2)),
        ],
        compiler_params=params(60),
        name="upper_solve",
    )(parent, incoming, slots, index, sep_rhs, sep_slots, sep_index, root_rhs, *operators)


def inverse_rows(index, extent):
    place = jnp.arange(index.shape[1], dtype=jnp.int32)[None, :, None]
    slot = jnp.arange(extent, dtype=jnp.int32)[None, None, :]
    return jnp.max(jnp.where(index[:, :, None] == slot, place, -1), axis=1)


def swap_cores(value):
    return lax.ppermute(value, "c", [(0, 1), (1, 0)])


def along_plane(value, step, first):
    pairs = []
    for y in range(NY):
        for x in range(NX):
            for c in range(NC):
                by_x = (c == 0) == first
                to_y, to_x = (y, (x + step) % NX) if by_x else ((y + step) % NY, x)
                pairs.append(((y * NX + x) * NC + c, (to_y * NX + to_x) * NC + c))
    return lax.ppermute(value, ("y", "x", "c"), pairs)


def gather_plane(value, first, beside):
    ahead = along_plane(value, 1, first)
    back = along_plane(value, -1, first)
    ahead, back, beside = lax.optimization_barrier((ahead, back, beside))
    return (value, ahead, back, along_plane(ahead, 1, first)), beside


def gather_line(separator_factor, y, x):
    mine = lax.dynamic_slice(separator_factor, (y, 8 * x, 0), (1, 8, 512))
    return lax.all_to_all(
        jnp.broadcast_to(mine, (NZ, 8, 512)), "z", split_axis=0, concat_axis=0, tiled=True
    )


def spread_line(line, beside_first, beside_second):
    parts = [line, along_plane(line, 1, True), along_plane(line, -1, True), along_plane(line, 2, True)]
    parts, beside_first = lax.optimization_barrier((parts, beside_first))
    rows = jnp.stack(parts)
    swapped = swap_cores(rows)
    own, (beside_second, swapped) = gather_plane(rows, False, (beside_second, swapped))
    other = (swapped, swap_cores(own[1]), swap_cores(own[2]))
    return own, other, beside_first, beside_second


def local(
    leaf_rhs,
    leaf_factor,
    pivot_count,
    parent,
    leaf_index,
    separator_rhs,
    separator_factor,
    separator_index,
    root_rhs,
    root_factor,
):
    rhs = leaf_rhs[0]
    slots = inverse_rows(leaf_index, 1024)[:, None, :]
    sep_slots = inverse_rows(separator_index, 512)[:, None, :]
    sep_rhs = jnp.transpose(separator_rhs[0], (1, 0, 2))
    y, x, c = lax.axis_index("y"), lax.axis_index("x"), lax.axis_index("c")
    place = jnp.stack([y, x, c]).astype(jnp.int32)
    line = lax.all_gather(join(leaf_factor[0], root_factor), ("z", "c"), axis=0, tiled=False)
    sep_line = gather_line(separator_factor, y, x)
    own_set, other_set, (sep_slots, sep_rhs), slots = spread_line(pack(sep_line), (sep_slots, sep_rhs), slots)

    border = leaf_border(pivot_count, rhs, line)
    far, line, border = lax.optimization_barrier((own_set[3], line, border))
    own_set, other_set = own_set[:3] + (far,), other_set + (swap_cores(far),)
    incoming = lax.all_to_all(
        border.reshape(16, 16, 512), ("y", "x"), split_axis=0, concat_axis=0, tiled=True
    )
    operators = upper_operators(place, own_set, other_set, line)
    down, sep_answer, root_answer = upper_solve(
        parent, incoming, slots, leaf_index[:, None, :], sep_rhs, sep_slots,
        separator_index[:, None, :], root_rhs[0], operators,
    )
    line, down = lax.optimization_barrier((line, down))
    received = lax.all_to_all(down, ("y", "x"), split_axis=0, concat_axis=0, tiled=True)
    part, high, low = leaf_pivot(pivot_count, rhs, line)
    leaf_answer = leaf_last(pivot_count, part, received.reshape(256, 512), high, low)
    return leaf_answer[None], jnp.transpose(sep_answer, (1, 0, 2))[None], root_answer[None]


def solution(mesh):
    fine = Mesh(mesh.devices.reshape(NY, NX, NZ, NC), ("y", "x", "z", "c"))
    leaf, src = ("y", "x"), ("z", "c")
    return jax.shard_map(
        local,
        mesh=fine,
        in_specs=(
            P(leaf, src, None),
            P(leaf, src, None),
            P(leaf),
            P(),
            P(),
            P(leaf, src, None, None),
            P(None, src, None),
            P(),
            P(leaf, src, None),
            P(src, None),
        ),
        out_specs=(P(leaf, src, None), P(leaf, src, None, None), P(leaf, src, None)),
        check_vma=False,
    )
```

```python
import jax
import jax.numpy as jnp
from jax import lax
from jax.experimental import pallas as pl
from jax.experimental.pallas import tpu as pltpu
from jax.sharding import Mesh, PartitionSpec as P

NY, NX, NZ, NC = 4, 4, 16, 2
F32, BF16 = jnp.float32, jnp.bfloat16
LANES = 128


def split2(value):
    high = value.astype(BF16)
    return high, (value - high.astype(F32)).astype(BF16)


def dot_nt(a, b):
    return lax.dot_general(a, b, (((1,), (1,)), ((), ())), preferred_element_type=F32)


def dot_nn(a, b):
    return lax.dot_general(a, b, (((1,), (0,)), ((), ())), preferred_element_type=F32)


def stack2(pair):
    return jnp.concatenate(pair, axis=0)


def stacked_products(dot, both, b):
    rows = both.shape[0] // 2
    first = dot(both, b[0])
    return first[:rows] + (first[rows:] + dot(both[:rows], b[1]))


def params(mebibytes):
    return pltpu.CompilerParams(vmem_limit_bytes=mebibytes * 1024 * 1024)


def full_vmem():
    return pl.BlockSpec(memory_space=pltpu.VMEM)


def full_smem():
    return pl.BlockSpec(memory_space=pltpu.SMEM)


def in_hbm():
    return pl.BlockSpec(memory_space=pltpu.HBM)


def anywhere():
    return pl.BlockSpec(memory_space=pl.ANY)


def start_all(copies):
    for copy in copies:
        copy.start()


def wait_all(copies):
    for copy in copies:
        copy.wait()


LEAF_ROWS, SHARD = 48, 56


def join_kernel(leaf_ref, root_ref, out_ref):
    out_ref[:LEAF_ROWS] = leaf_ref[...]
    out_ref[LEAF_ROWS:, :512] = root_ref[:8]
    out_ref[LEAF_ROWS:, 512:] = root_ref[8:]


def join(leaf, root):
    return pl.pallas_call(
        join_kernel,
        out_shape=jax.ShapeDtypeStruct((SHARD, 1024), F32),
        in_specs=[full_vmem()] * 2,
        out_specs=full_vmem(),
        compiler_params=params(60),
        name="join",
    )(leaf, root)


def leaf_copy(line_ref, buffer, first, count, sem):
    return pltpu.make_async_copy(line_ref.at[pl.ds(first, count), pl.ds(0, LEAF_ROWS), :], buffer, sem)


def leaf_border_kernel(count_ref, rhs_hbm, line_ref, border_ref, rhs_ref, buffer, sem, rhs_sem):
    copies = [
        leaf_copy(line_ref, buffer.at[pl.ds(0, 6)], 21, 6, sem.at[0]),
        leaf_copy(line_ref, buffer.at[pl.ds(6, 5)], 27, 5, sem.at[1]),
    ]
    load = pltpu.make_async_copy(rhs_hbm, rhs_ref, rhs_sem)
    load.start()
    start_all(copies)
    load.wait()
    cols = lax.broadcasted_iota(jnp.int32, rhs_ref.shape, 1)
    rhs = stack2(split2(jnp.where(cols < count_ref[0], rhs_ref[...], 0.0)))
    for block in range(2):
        copies[block].wait()
        rows = buffer[5 * block : 5 * block + 6].reshape(288, 1024)[16 * (block + 1) : 16 * (block + 1) + 256]
        border_ref[:, 256 * block : 256 * (block + 1)] = stacked_products(dot_nt, rhs, split2(rows))


def leaf_border(count, rhs, line):
    return pl.pallas_call(
        leaf_border_kernel,
        out_shape=jax.ShapeDtypeStruct((256, 512), F32),
        in_specs=[full_smem(), in_hbm(), in_hbm()],
        out_specs=full_vmem(),
        scratch_shapes=[
            pltpu.VMEM((256, 1024), F32),
            pltpu.VMEM((11, 48, 1024), F32),
            pltpu.SemaphoreType.DMA((2,)),
            pltpu.SemaphoreType.DMA,
        ],
        compiler_params=params(60),
        name="leaf_border",
    )(count, rhs, line)


def leaf_pivot_kernel(
    count_ref, rhs_hbm, line_ref,
    part_hbm, border_high_hbm, border_low_hbm,
    rhs_ref, buffer, border_buffer, high_ref, low_ref, part_ref, border_high_ref, border_low_ref, sem, out_sem,
):
    copy = leaf_copy(line_ref, buffer, 0, 22, sem.at[0])
    border_copy = leaf_copy(line_ref, border_buffer, 21, 11, sem.at[1])
    load = pltpu.make_async_copy(rhs_hbm, rhs_ref, sem.at[2])
    load.start()
    copy.start()
    border_copy.start()
    count = count_ref[0]
    load.wait()
    cols = lax.broadcasted_iota(jnp.int32, rhs_ref.shape, 1)
    rhs = stack2(split2(jnp.where(cols < count, rhs_ref[...], 0.0)))
    copy.wait()
    top = buffer[...].reshape(1056, 1024)
    solved = []
    for block in range(4):
        first, wide = 256 * block, 256 * (block + 1)
        rows = first + lax.broadcasted_iota(jnp.int32, (256, wide), 0)
        columns = lax.broadcasted_iota(jnp.int32, (256, wide), 1)
        values = jnp.where(columns < rows, top[first:wide, :wide], 0.0)
        values = jnp.where(columns == rows, 1.0, values)
        values = jnp.where(rows < count, values, 0.0)
        high, low = split2(values)
        high_ref[first:wide, :wide] = high
        low_ref[first:wide, :wide] = low
        solved.append(stacked_products(dot_nt, rhs[:, :wide], (high, low)))
    solved = stack2(split2(jnp.concatenate(solved, axis=1)))
    border_copy.wait()
    border = border_buffer[...].reshape(528, 1024)
    stores = []
    for block in range(4):
        first, wide = 256 * block, 256 * (block + 1)
        border_high_ref[block], border_low_ref[block] = split2(border[16:, first:wide])
        part_ref[block] = stacked_products(
            dot_nn,
            solved[:, first:],
            (high_ref[first:, first:wide], low_ref[first:, first:wide]),
        )
        stores += [
            pltpu.make_async_copy(part_ref.at[block], part_hbm.at[block], out_sem.at[block, 0]),
            pltpu.make_async_copy(border_high_ref.at[block], border_high_hbm.at[block], out_sem.at[block, 1]),
            pltpu.make_async_copy(border_low_ref.at[block], border_low_hbm.at[block], out_sem.at[block, 2]),
        ]
        start_all(stores[-3:])
    wait_all(stores)


def leaf_pivot(count, rhs, line):
    return pl.pallas_call(
        leaf_pivot_kernel,
        out_shape=(
            jax.ShapeDtypeStruct((4, 256, 256), F32),
            jax.ShapeDtypeStruct((4, 512, 256), BF16),
            jax.ShapeDtypeStruct((4, 512, 256), BF16),
        ),
        in_specs=[full_smem(), in_hbm(), in_hbm()],
        out_specs=(in_hbm(),) * 3,
        scratch_shapes=[
            pltpu.VMEM((256, 1024), F32),
            pltpu.VMEM((22, 48, 1024), F32),
            pltpu.VMEM((11, 48, 1024), F32),
            pltpu.VMEM((1024, 1024), BF16),
            pltpu.VMEM((1024, 1024), BF16),
            pltpu.VMEM((4, 256, 256), F32),
            pltpu.VMEM((4, 512, 256), BF16),
            pltpu.VMEM((4, 512, 256), BF16),
            pltpu.SemaphoreType.DMA((3,)),
            pltpu.SemaphoreType.DMA((4, 3)),
        ],
        compiler_params=params(60),
        name="leaf_pivot",
    )(count, rhs, line)


def leaf_last_kernel(
    count_ref, part_hbm, border_hbm, high_hbm, low_hbm, out_hbm,
    part_ref, border_ref, high_ref, low_ref, out_ref, sem, border_sem, out_sem,
):
    load = pltpu.make_async_copy(border_hbm, border_ref, border_sem)
    load.start()
    copies = [
        [
            pltpu.make_async_copy(source.at[block], to.at[block], sem.at[block, at])
            for at, (source, to) in enumerate(((high_hbm, high_ref), (low_hbm, low_ref), (part_hbm, part_ref)))
        ]
        for block in range(4)
    ]
    for group in copies:
        start_all(group)
    load.wait()
    border = stack2(split2(border_ref[...]))
    stores = []
    for block in range(4):
        wait_all(copies[block])
        answer = part_ref[block] + stacked_products(dot_nn, border, (high_ref[block], low_ref[block]))
        cols = 256 * block + lax.broadcasted_iota(jnp.int32, answer.shape, 1)
        out_ref[block] = jnp.where(cols < count_ref[0], answer, 0.0)
        stores.append(
            pltpu.make_async_copy(out_ref.at[block], out_hbm.at[:, pl.ds(256 * block, 256)], out_sem.at[block])
        )
        stores[-1].start()
    wait_all(stores)


def leaf_last(count, part, border, high, low):
    return pl.pallas_call(
        leaf_last_kernel,
        out_shape=jax.ShapeDtypeStruct((256, 1024), F32),
        in_specs=[full_smem()] + [in_hbm()] * 4,
        out_specs=in_hbm(),
        scratch_shapes=[
            pltpu.VMEM((4, 256, 256), F32),
            pltpu.VMEM((256, 512), F32),
            pltpu.VMEM((4, 512, 256), BF16),
            pltpu.VMEM((4, 512, 256), BF16),
            pltpu.VMEM((4, 256, 256), F32),
            pltpu.SemaphoreType.DMA((4, 3)),
            pltpu.SemaphoreType.DMA,
            pltpu.SemaphoreType.DMA((4,)),
        ],
        compiler_params=params(60),
        name="leaf_last",
    )(count, part, border, high, low)


LANE_GATHER = lax.GatherDimensionNumbers(
    offset_dims=(),
    collapsed_slice_dims=(1,),
    start_index_map=(1,),
    operand_batching_dims=(0,),
    start_indices_batching_dims=(0,),
)


def take_lanes(value, lane):
    return lax.gather(
        value, lane[..., None], LANE_GATHER, slice_sizes=(1, 1), mode=lax.GatherScatterMode.PROMISE_IN_BOUNDS
    )


def pick(values, index_row):
    out = []
    for block in range(index_row.shape[1] // LANES):
        index = jnp.broadcast_to(index_row[:, block * LANES : (block + 1) * LANES], (8, LANES))
        lane, found = index & (LANES - 1), index >= 0
        bits = [(index & (LANES << bit)) != 0 for bit in range(len(values).bit_length() - 1)]
        halves = []
        for half in range(2):
            level = [take_lanes(value[8 * half : 8 * half + 8], lane) for value in values]
            for bit in bits:
                level = [jnp.where(bit, odd, even) for even, odd in zip(level[::2], level[1::2])]
            halves.append(jnp.where(found, level[0], 0.0))
        out.append(jnp.concatenate(halves, axis=0))
    return out


def blocks(value):
    return [value[:, at * LANES : (at + 1) * LANES] for at in range(value.shape[1] // LANES)]


OFFSETS = (0, -1, 1, -2)
TILES = [min(4, z // 2 + 1) for z in range(NZ)]
FIRST_TILE = [sum(TILES[:z]) for z in range(NZ)]
PACKED = sum(TILES)


def pack_kernel(line_ref, out_ref):
    for z in range(NZ):
        for tile in range(TILES[z]):
            out_ref[FIRST_TILE[z] + tile] = line_ref[z, :, tile * LANES : (tile + 1) * LANES]


def pack(line):
    return pl.pallas_call(
        pack_kernel,
        out_shape=jax.ShapeDtypeStruct((PACKED, 8, LANES), F32),
        in_specs=[full_vmem()],
        out_specs=full_vmem(),
        compiler_params=params(60),
        name="pack",
    )(line)


def upper_operator_kernel(place_ref, *refs):
    own_refs, other_refs, line_ref = refs[:4], refs[4:8], refs[8]
    high_hbm, low_hbm, root_high_hbm, root_low_hbm = refs[9:13]
    buffer, root_buffer, high_ref, low_ref, root_high_ref, root_low_ref, sem, root_sem, out_sem = refs[13:]
    y, x, c = place_ref[0], place_ref[1], place_ref[2]
    for piece_refs, parity in ((own_refs, c), (other_refs, 1 - c)):
        for outer in range(4):
            for inner in range(4):
                source = piece_refs[outer].at[inner]
                along_y = jnp.where(parity == 0, OFFSETS[outer], OFFSETS[inner])
                along_x = jnp.where(parity == 0, OFFSETS[inner], OFFSETS[outer])
                group = jnp.where(parity == 0, outer, inner)
                to_y = lax.rem(y + along_y + 8, 4)
                to_x = lax.rem(x + along_x + 8, 4)
                pltpu.make_async_copy(source, buffer.at[to_y, to_x, parity], sem.at[group]).start()
    root_copies = [
        pltpu.make_async_copy(
            line_ref.at[:, pl.ds(LEAF_ROWS, 8), pl.ds(512 * half, 512)],
            root_buffer.at[:, pl.ds(8 * half, 8), :],
            root_sem.at[half],
        )
        for half in range(2)
    ]
    start_all(root_copies)

    def out_copies(group):
        offset = jnp.int32(OFFSETS[0])
        for at in range(1, 4):
            offset = jnp.where(group == at, OFFSETS[at], offset)
        sep = lax.rem(y + offset + 8, 4)
        return sep, [
            pltpu.make_async_copy(high_ref.at[sep], high_hbm.at[sep], out_sem.at[2 * group]),
            pltpu.make_async_copy(low_ref.at[sep], low_hbm.at[sep], out_sem.at[2 * group + 1]),
        ]

    def one_group(group, _):
        for _ in range(8):
            pltpu.make_async_copy(own_refs[0].at[0], buffer.at[0, 0, 0], sem.at[group]).wait()
        sep, copies = out_copies(group)

        def rows(parity, first, tiles):
            return jnp.concatenate([
                jnp.concatenate([buffer[sep, q, parity, first + tile] for tile in range(tiles)], axis=1)
                for q in range(4)
            ], axis=0)

        for z in range(8):
            width = TILES[z] * LANES
            for parity in range(2):
                first_row = 32 * (2 * z + parity)
                row_ids = first_row + lax.broadcasted_iota(jnp.int32, (32, width), 0)
                col_ids = lax.broadcasted_iota(jnp.int32, (32, width), 1)
                value = lower_unit(rows(parity, FIRST_TILE[z], TILES[z]), row_ids, col_ids)
                high, low = split2(value)
                to = slice(first_row, first_row + 32)
                high_ref[sep, to, :width] = high
                low_ref[sep, to, :width] = low
                if width < 512:
                    high_ref[sep, to, width:] = jnp.zeros((32, 512 - width), BF16)
                    low_ref[sep, to, width:] = jnp.zeros((32, 512 - width), BF16)

        def border_rows(z, _):
            for parity in range(2):
                to = pl.ds(pl.multiple_of((2 * z + parity) * 32, 32), 32)
                high_ref[sep, to], low_ref[sep, to] = split2(rows(parity, FIRST_TILE[8] + 4 * (z - 8), 4))
            return 0

        lax.fori_loop(8, 16, border_rows, 0)
        start_all(copies)
        return 0

    lax.fori_loop(0, 4, one_group, 0)
    wait_all(root_copies)
    row_ids = lax.broadcasted_iota(jnp.int32, (512, 512), 0)
    col_ids = lax.broadcasted_iota(jnp.int32, (512, 512), 1)
    value = lower_unit(root_buffer[...].reshape(512, 512), row_ids, col_ids)
    root_high_ref[...], root_low_ref[...] = split2(value)
    root_stores = [
        pltpu.make_async_copy(root_high_ref, root_high_hbm, out_sem.at[8]),
        pltpu.make_async_copy(root_low_ref, root_low_hbm, out_sem.at[9]),
    ]
    start_all(root_stores)
    for group in range(4):
        wait_all(out_copies(group)[1])
    wait_all(root_stores)


def lower_unit(value, row_ids, col_ids):
    return jnp.where(col_ids == row_ids, 1.0, jnp.where(col_ids < row_ids, value, 0.0))


def upper_operators(place, own, other, line):
    return pl.pallas_call(
        upper_operator_kernel,
        out_shape=(
            jax.ShapeDtypeStruct((4, 1024, 512), BF16),
            jax.ShapeDtypeStruct((4, 1024, 512), BF16),
            jax.ShapeDtypeStruct((512, 512), BF16),
            jax.ShapeDtypeStruct((512, 512), BF16),
        ),
        in_specs=[full_smem()] + [in_hbm()] * 9,
        out_specs=(in_hbm(),) * 4,
        scratch_shapes=[
            pltpu.VMEM((NY, NX, NC, PACKED, 8, LANES), F32),
            pltpu.VMEM((32, 16, 512), F32),
            pltpu.VMEM((4, 1024, 512), BF16),
            pltpu.VMEM((4, 1024, 512), BF16),
            pltpu.VMEM((512, 512), BF16),
            pltpu.VMEM((512, 512), BF16),
            pltpu.SemaphoreType.DMA((4,)),
            pltpu.SemaphoreType.DMA((2,)),
            pltpu.SemaphoreType.DMA((10,)),
        ],
        compiler_params=params(60),
        name="upper_operators",
    )(place, *own, *other, line)


def upper_kernel(
    parent_ref, incoming_hbm, slot_hbm, index_hbm, sep_rhs_hbm, sep_slot_hbm, sep_index_hbm, root_rhs_hbm,
    high_hbm, low_hbm, root_high_hbm, root_low_hbm,
    down_ref, sep_out_ref, root_out_ref,
    incoming_ref, slot_ref, index_ref, sep_rhs_ref, sep_slot_ref, sep_index_ref, root_rhs_ref,
    updates, solved, full, high_ref, low_ref, root_high_ref, root_low_ref, first_sem, sem,
):
    first_loads = [
        pltpu.make_async_copy(slot_hbm, slot_ref, first_sem.at[0]),
        pltpu.make_async_copy(incoming_hbm.at[pl.ds(0, 4)], incoming_ref.at[pl.ds(0, 4)], first_sem.at[1]),
        pltpu.make_async_copy(incoming_hbm.at[pl.ds(4, 12)], incoming_ref.at[pl.ds(4, 12)], first_sem.at[2]),
    ]
    small_loads = [
        pltpu.make_async_copy(source, to, first_sem.at[3 + at])
        for at, (source, to) in enumerate((
            (sep_rhs_hbm, sep_rhs_ref), (sep_slot_hbm, sep_slot_ref), (root_rhs_hbm, root_rhs_ref),
            (sep_index_hbm, sep_index_ref), (index_hbm, index_ref),
        ))
    ]
    start_all(first_loads + small_loads)
    loads = []
    for sep in range(4):
        loads.append([
            pltpu.make_async_copy(high_hbm.at[sep], high_ref.at[sep], sem.at[sep, 0]),
            pltpu.make_async_copy(low_hbm.at[sep], low_ref.at[sep], sem.at[sep, 1]),
        ])
    loads.append([
        pltpu.make_async_copy(root_high_hbm, root_high_ref, sem.at[4, 0]),
        pltpu.make_async_copy(root_low_hbm, root_low_ref, sem.at[4, 1]),
    ])
    for group in loads:
        start_all(group)
    updates[...] = jnp.zeros(updates.shape, F32)

    def spread(leaf, _):
        to = parent_ref[leaf]
        picked = pick(blocks(incoming_ref[leaf]), slot_ref[pl.ds(leaf, 1), :])
        for at, value in enumerate(picked):
            part = slice(at * LANES, (at + 1) * LANES)
            updates[to, :, part] = updates[to, :, part] + value
        return 0

    wait_all(first_loads[:2])
    lax.fori_loop(0, 4, spread, 0, unroll=4)
    first_loads[2].wait()
    lax.fori_loop(4, 16, spread, 0, unroll=4)
    wait_all(small_loads)
    root_total = root_rhs_ref[...]
    for sep in range(4):
        wait_all(loads[sep])
        pivot = stack2(split2(sep_rhs_ref[sep] + updates[sep, :, :512]))
        forward = stacked_products(dot_nt, pivot, (high_ref[sep], low_ref[sep]))
        solved[sep] = forward[:, :512]
        border = forward[:, 512:] + updates[sep, :, 512:]
        root_total = root_total + jnp.concatenate(pick(blocks(border), sep_slot_ref[sep : sep + 1, :]), axis=1)
    wait_all(loads[4])
    root = (root_high_ref[...], root_low_ref[...])
    root_solved = stacked_products(dot_nt, stack2(split2(root_total)), root)
    root_answer = stacked_products(dot_nn, stack2(split2(root_solved)), root)
    root_out_ref[...] = root_answer
    for sep in range(4):
        border = jnp.concatenate(pick(blocks(root_answer), sep_index_ref[sep : sep + 1, :]), axis=1)
        joined = stack2(split2(jnp.concatenate([solved[sep], border], axis=1)))
        answer = stacked_products(dot_nn, joined, (high_ref[sep], low_ref[sep]))
        sep_out_ref[sep] = answer
        full[sep, :, :512] = answer
        full[sep, :, 512:] = border

    def gather(leaf, _):
        picked = pick(blocks(full[parent_ref[leaf]]), index_ref[pl.ds(leaf, 1), :])
        down_ref[leaf] = jnp.concatenate(picked, axis=1)
        return 0

    lax.fori_loop(0, 16, gather, 0, unroll=4)


def upper_solve(parent, incoming, slots, index, sep_rhs, sep_slots, sep_index, root_rhs, operators):
    return pl.pallas_call(
        upper_kernel,
        out_shape=(
            jax.ShapeDtypeStruct((16, 16, 512), F32),
            jax.ShapeDtypeStruct((4, 16, 512), F32),
            jax.ShapeDtypeStruct((16, 512), F32),
        ),
        in_specs=[full_smem()] + [in_hbm()] * 11,
        out_specs=(full_vmem(),) * 3,
        scratch_shapes=[
            pltpu.VMEM((16, 16, 512), F32),
            pltpu.VMEM((16, 1024), jnp.int32),
            pltpu.VMEM((16, 512), jnp.int32),
            pltpu.VMEM((4, 16, 512), F32),
            pltpu.VMEM((4, 512), jnp.int32),
            pltpu.VMEM((4, 512), jnp.int32),
            pltpu.VMEM((16, 512), F32),
            pltpu.VMEM((4, 16, 1024), F32),
            pltpu.VMEM((4, 16, 512), F32),
            pltpu.VMEM((4, 16, 1024), F32),
            pltpu.VMEM((4, 1024, 512), BF16),
            pltpu.VMEM((4, 1024, 512), BF16),
            pltpu.VMEM((512, 512), BF16),
            pltpu.VMEM((512, 512), BF16),
            pltpu.SemaphoreType.DMA((8,)),
            pltpu.SemaphoreType.DMA((5, 2)),
        ],
        compiler_params=params(60),
        name="upper_solve",
    )(parent, incoming, slots, index, sep_rhs, sep_slots, sep_index, root_rhs, *operators)


def inverse_rows(index, extent):
    place = jnp.arange(index.shape[1], dtype=jnp.int32)[None, :, None]
    slot = jnp.arange(extent, dtype=jnp.int32)[None, None, :]
    return jnp.max(jnp.where(index[:, :, None] == slot, place, -1), axis=1)


def swap_cores(value):
    return lax.ppermute(value, "c", [(0, 1), (1, 0)])


def along_plane(value, step, first):
    pairs = []
    for y in range(NY):
        for x in range(NX):
            for c in range(NC):
                by_x = (c == 0) == first
                to_y, to_x = (y, (x + step) % NX) if by_x else ((y + step) % NY, x)
                pairs.append(((y * NX + x) * NC + c, (to_y * NX + to_x) * NC + c))
    return lax.ppermute(value, ("y", "x", "c"), pairs)


def gather_plane(value, first, beside):
    ahead = along_plane(value, 1, first)
    back = along_plane(value, -1, first)
    ahead, back, beside = lax.optimization_barrier((ahead, back, beside))
    return (value, ahead, back, along_plane(ahead, 1, first)), beside


def gather_line(separator_factor, y, x):
    mine = lax.dynamic_slice(separator_factor, (y, 8 * x, 0), (1, 8, 512))
    return lax.all_to_all(
        jnp.broadcast_to(mine, (NZ, 8, 512)), "z", split_axis=0, concat_axis=0, tiled=True
    )


def spread_line(line, beside_first, beside_second):
    parts = [line, along_plane(line, 1, True), along_plane(line, -1, True), along_plane(line, 2, True)]
    parts, beside_first = lax.optimization_barrier((parts, beside_first))
    rows = jnp.stack(parts)
    swapped = swap_cores(rows)
    own, (beside_second, swapped) = gather_plane(rows, False, (beside_second, swapped))
    other = (swapped, swap_cores(own[1]), swap_cores(own[2]))
    return own, other, beside_first, beside_second


def local(
    leaf_rhs,
    leaf_factor,
    pivot_count,
    parent,
    leaf_index,
    separator_rhs,
    separator_factor,
    separator_index,
    root_rhs,
    root_factor,
):
    rhs = leaf_rhs[0]
    slots = inverse_rows(leaf_index, 1024)
    sep_slots = inverse_rows(separator_index, 512)
    sep_rhs = jnp.transpose(separator_rhs[0], (1, 0, 2))
    y, x, c = lax.axis_index("y"), lax.axis_index("x"), lax.axis_index("c")
    place = jnp.stack([y, x, c]).astype(jnp.int32)
    line = lax.all_gather(join(leaf_factor[0], root_factor), ("z", "c"), axis=0, tiled=False)
    sep_line = gather_line(separator_factor, y, x)
    own_set, other_set, (sep_slots, sep_rhs), slots = spread_line(pack(sep_line), (sep_slots, sep_rhs), slots)

    border = leaf_border(pivot_count, rhs, line)
    far, line, border = lax.optimization_barrier((own_set[3], line, border))
    own_set, other_set = own_set[:3] + (far,), other_set + (swap_cores(far),)
    incoming = lax.all_to_all(
        border.reshape(16, 16, 512), ("y", "x"), split_axis=0, concat_axis=0, tiled=True
    )
    operators = upper_operators(place, own_set, other_set, line)
    down, sep_answer, root_answer = upper_solve(
        parent, incoming, slots, leaf_index, sep_rhs, sep_slots,
        separator_index, root_rhs[0], operators,
    )
    line, down = lax.optimization_barrier((line, down))
    received = lax.all_to_all(down, ("y", "x"), split_axis=0, concat_axis=0, tiled=True)
    part, high, low = leaf_pivot(pivot_count, rhs, line)
    leaf_answer = leaf_last(pivot_count, part, received.reshape(256, 512), high, low)
    return leaf_answer[None], jnp.transpose(sep_answer, (1, 0, 2))[None], root_answer[None]


def solution(mesh):
    fine = Mesh(mesh.devices.reshape(NY, NX, NZ, NC), ("y", "x", "z", "c"))
    leaf, src = ("y", "x"), ("z", "c")
    return jax.shard_map(
        local,
        mesh=fine,
        in_specs=(
            P(leaf, src, None),
            P(leaf, src, None),
            P(leaf),
            P(),
            P(),
            P(leaf, src, None, None),
            P(None, src, None),
            P(),
            P(leaf, src, None),
            P(src, None),
        ),
        out_specs=(P(leaf, src, None), P(leaf, src, None, None), P(leaf, src, None)),
        check_vma=False,
    )
```

```python
import jax
import jax.numpy as jnp
from jax import lax
from jax.experimental import pallas as pl
from jax.experimental.pallas import tpu as pltpu
from jax.sharding import Mesh, PartitionSpec as P

NY, NX, NZ, NC = 4, 4, 16, 2
F32, BF16 = jnp.float32, jnp.bfloat16
LANES = 128


def split2(value):
    high = value.astype(BF16)
    return high, (value - high.astype(F32)).astype(BF16)


def dot_nt(a, b):
    return lax.dot_general(a, b, (((1,), (1,)), ((), ())), preferred_element_type=F32)


def dot_nn(a, b):
    return lax.dot_general(a, b, (((1,), (0,)), ((), ())), preferred_element_type=F32)


def stack2(pair):
    return jnp.concatenate(pair, axis=0)


def stacked_products(dot, both, b):
    rows = both.shape[0] // 2
    first = dot(both, b[0])
    return first[:rows] + (first[rows:] + dot(both[:rows], b[1]))


def params(mebibytes):
    return pltpu.CompilerParams(vmem_limit_bytes=mebibytes * 1024 * 1024)


def full_vmem():
    return pl.BlockSpec(memory_space=pltpu.VMEM)


def full_smem():
    return pl.BlockSpec(memory_space=pltpu.SMEM)


def in_hbm():
    return pl.BlockSpec(memory_space=pltpu.HBM)


def anywhere():
    return pl.BlockSpec(memory_space=pl.ANY)


def start_all(copies):
    for copy in copies:
        copy.start()


def wait_all(copies):
    for copy in copies:
        copy.wait()


LEAF_ROWS, SHARD = 48, 56


def join_kernel(leaf_ref, root_ref, out_ref):
    out_ref[:LEAF_ROWS] = leaf_ref[...]
    out_ref[LEAF_ROWS:, :512] = root_ref[:8]
    out_ref[LEAF_ROWS:, 512:] = root_ref[8:]


def join(leaf, root):
    return pl.pallas_call(
        join_kernel,
        out_shape=jax.ShapeDtypeStruct((SHARD, 1024), F32),
        in_specs=[full_vmem()] * 2,
        out_specs=full_vmem(),
        compiler_params=params(60),
        name="join",
    )(leaf, root)


def leaf_copy(line_ref, buffer, first, count, sem):
    return pltpu.make_async_copy(line_ref.at[pl.ds(first, count), pl.ds(0, LEAF_ROWS), :], buffer, sem)


def leaf_border_kernel(count_ref, rhs_hbm, line_ref, border_ref, rhs_ref, buffer, sem, rhs_sem):
    copy = leaf_copy(line_ref, buffer, 21, 11, sem)
    load = pltpu.make_async_copy(rhs_hbm, rhs_ref, rhs_sem)
    load.start()
    copy.start()
    load.wait()
    cols = lax.broadcasted_iota(jnp.int32, rhs_ref.shape, 1)
    rhs = stack2(split2(jnp.where(cols < count_ref[0], rhs_ref[...], 0.0)))
    copy.wait()
    rows = buffer[...].reshape(528, 1024)
    for block in range(2):
        first = 16 + 256 * block
        border_ref[:, 256 * block : 256 * (block + 1)] = stacked_products(
            dot_nt, rhs, split2(rows[first : first + 256])
        )


def leaf_border(count, rhs, line):
    return pl.pallas_call(
        leaf_border_kernel,
        out_shape=jax.ShapeDtypeStruct((256, 512), F32),
        in_specs=[full_smem(), in_hbm(), in_hbm()],
        out_specs=full_vmem(),
        scratch_shapes=[
            pltpu.VMEM((256, 1024), F32),
            pltpu.VMEM((11, 48, 1024), F32),
            pltpu.SemaphoreType.DMA,
            pltpu.SemaphoreType.DMA,
        ],
        compiler_params=params(60),
        name="leaf_border",
    )(count, rhs, line)


def leaf_pivot_kernel(
    count_ref, rhs_hbm, line_ref,
    part_hbm, border_high_hbm, border_low_hbm,
    rhs_ref, buffer, border_buffer, high_ref, low_ref, part_ref, border_high_ref, border_low_ref, sem, out_sem,
):
    copy = leaf_copy(line_ref, buffer, 0, 22, sem.at[0])
    border_copy = leaf_copy(line_ref, border_buffer, 21, 11, sem.at[1])
    load = pltpu.make_async_copy(rhs_hbm, rhs_ref, sem.at[2])
    load.start()
    copy.start()
    border_copy.start()
    count = count_ref[0]
    load.wait()
    cols = lax.broadcasted_iota(jnp.int32, rhs_ref.shape, 1)
    rhs = stack2(split2(jnp.where(cols < count, rhs_ref[...], 0.0)))
    copy.wait()
    top = buffer[...].reshape(1056, 1024)
    solved = []
    for block in range(4):
        first, wide = 256 * block, 256 * (block + 1)
        rows = first + lax.broadcasted_iota(jnp.int32, (256, wide), 0)
        columns = lax.broadcasted_iota(jnp.int32, (256, wide), 1)
        values = jnp.where(columns < rows, top[first:wide, :wide], 0.0)
        values = jnp.where(columns == rows, 1.0, values)
        values = jnp.where(rows < count, values, 0.0)
        high, low = split2(values)
        high_ref[first:wide, :wide] = high
        low_ref[first:wide, :wide] = low
        solved.append(stacked_products(dot_nt, rhs[:, :wide], (high, low)))
    solved = stack2(split2(jnp.concatenate(solved, axis=1)))
    border_copy.wait()
    border = border_buffer[...].reshape(528, 1024)
    stores = []
    for block in range(4):
        first, wide = 256 * block, 256 * (block + 1)
        border_high_ref[block], border_low_ref[block] = split2(border[16:, first:wide])
        part_ref[block] = stacked_products(
            dot_nn,
            solved[:, first:],
            (high_ref[first:, first:wide], low_ref[first:, first:wide]),
        )
        stores += [
            pltpu.make_async_copy(part_ref.at[block], part_hbm.at[block], out_sem.at[block, 0]),
            pltpu.make_async_copy(border_high_ref.at[block], border_high_hbm.at[block], out_sem.at[block, 1]),
            pltpu.make_async_copy(border_low_ref.at[block], border_low_hbm.at[block], out_sem.at[block, 2]),
        ]
        start_all(stores[-3:])
    wait_all(stores)


def leaf_pivot(count, rhs, line):
    return pl.pallas_call(
        leaf_pivot_kernel,
        out_shape=(
            jax.ShapeDtypeStruct((4, 256, 256), F32),
            jax.ShapeDtypeStruct((4, 512, 256), BF16),
            jax.ShapeDtypeStruct((4, 512, 256), BF16),
        ),
        in_specs=[full_smem(), in_hbm(), in_hbm()],
        out_specs=(in_hbm(),) * 3,
        scratch_shapes=[
            pltpu.VMEM((256, 1024), F32),
            pltpu.VMEM((22, 48, 1024), F32),
            pltpu.VMEM((11, 48, 1024), F32),
            pltpu.VMEM((1024, 1024), BF16),
            pltpu.VMEM((1024, 1024), BF16),
            pltpu.VMEM((4, 256, 256), F32),
            pltpu.VMEM((4, 512, 256), BF16),
            pltpu.VMEM((4, 512, 256), BF16),
            pltpu.SemaphoreType.DMA((3,)),
            pltpu.SemaphoreType.DMA((4, 3)),
        ],
        compiler_params=params(60),
        name="leaf_pivot",
    )(count, rhs, line)


def leaf_last_kernel(
    count_ref, part_hbm, border_ref, high_hbm, low_hbm, out_hbm,
    part_ref, high_ref, low_ref, out_ref, sem, out_sem,
):
    copies = [
        [
            pltpu.make_async_copy(source.at[block], to.at[block], sem.at[block, at])
            for at, (source, to) in enumerate(((high_hbm, high_ref), (low_hbm, low_ref), (part_hbm, part_ref)))
        ]
        for block in range(4)
    ]
    for group in copies:
        start_all(group)
    border = stack2(split2(border_ref[...]))
    stores = []
    for block in range(4):
        wait_all(copies[block])
        answer = part_ref[block] + stacked_products(dot_nn, border, (high_ref[block], low_ref[block]))
        cols = 256 * block + lax.broadcasted_iota(jnp.int32, answer.shape, 1)
        out_ref[block] = jnp.where(cols < count_ref[0], answer, 0.0)
        stores.append(
            pltpu.make_async_copy(out_ref.at[block], out_hbm.at[:, pl.ds(256 * block, 256)], out_sem.at[block])
        )
        stores[-1].start()
    wait_all(stores)


def leaf_last(count, part, border, high, low):
    return pl.pallas_call(
        leaf_last_kernel,
        out_shape=jax.ShapeDtypeStruct((256, 1024), F32),
        in_specs=[full_smem(), in_hbm(), full_vmem(), in_hbm(), in_hbm()],
        out_specs=in_hbm(),
        scratch_shapes=[
            pltpu.VMEM((4, 256, 256), F32),
            pltpu.VMEM((4, 512, 256), BF16),
            pltpu.VMEM((4, 512, 256), BF16),
            pltpu.VMEM((4, 256, 256), F32),
            pltpu.SemaphoreType.DMA((4, 3)),
            pltpu.SemaphoreType.DMA((4,)),
        ],
        compiler_params=params(59),
        name="leaf_last",
    )(count, part, border, high, low)


LANE_GATHER = lax.GatherDimensionNumbers(
    offset_dims=(),
    collapsed_slice_dims=(1,),
    start_index_map=(1,),
    operand_batching_dims=(0,),
    start_indices_batching_dims=(0,),
)


def take_lanes(value, lane):
    return lax.gather(
        value, lane[..., None], LANE_GATHER, slice_sizes=(1, 1), mode=lax.GatherScatterMode.PROMISE_IN_BOUNDS
    )


def pick(values, index_row):
    out = []
    for block in range(index_row.shape[1] // LANES):
        index = jnp.broadcast_to(index_row[:, block * LANES : (block + 1) * LANES], (8, LANES))
        lane, found = index & (LANES - 1), index >= 0
        bits = [(index & (LANES << bit)) != 0 for bit in range(len(values).bit_length() - 1)]
        halves = []
        for half in range(2):
            level = [take_lanes(value[8 * half : 8 * half + 8], lane) for value in values]
            for bit in bits:
                level = [jnp.where(bit, odd, even) for even, odd in zip(level[::2], level[1::2])]
            halves.append(jnp.where(found, level[0], 0.0))
        out.append(jnp.concatenate(halves, axis=0))
    return out


def blocks(value):
    return [value[:, at * LANES : (at + 1) * LANES] for at in range(value.shape[1] // LANES)]


OFFSETS = (0, -1, 1, -2)
TILES = [min(4, z // 2 + 1) for z in range(NZ)]
FIRST_TILE = [sum(TILES[:z]) for z in range(NZ)]
PACKED = sum(TILES)


def pack_kernel(line_ref, out_ref):
    for z in range(NZ):
        for tile in range(TILES[z]):
            out_ref[FIRST_TILE[z] + tile] = line_ref[z, :, tile * LANES : (tile + 1) * LANES]


def pack(line):
    return pl.pallas_call(
        pack_kernel,
        out_shape=jax.ShapeDtypeStruct((PACKED, 8, LANES), F32),
        in_specs=[full_vmem()],
        out_specs=full_vmem(),
        compiler_params=params(60),
        name="pack",
    )(line)


def upper_operator_kernel(place_ref, *refs):
    own_refs, other_refs, line_ref = refs[:4], refs[4:8], refs[8]
    high_hbm, low_hbm, root_high_hbm, root_low_hbm = refs[9:13]
    buffer, root_buffer, high_ref, low_ref, root_high_ref, root_low_ref, sem, root_sem, out_sem = refs[13:]
    y, x, c = place_ref[0], place_ref[1], place_ref[2]
    for piece_refs, parity in ((own_refs, c), (other_refs, 1 - c)):
        for outer in range(4):
            for inner in range(4):
                source = piece_refs[outer].at[inner]
                along_y = jnp.where(parity == 0, OFFSETS[outer], OFFSETS[inner])
                along_x = jnp.where(parity == 0, OFFSETS[inner], OFFSETS[outer])
                group = jnp.where(parity == 0, outer, inner)
                to_y = lax.rem(y + along_y + 8, 4)
                to_x = lax.rem(x + along_x + 8, 4)
                pltpu.make_async_copy(source, buffer.at[to_y, to_x, parity], sem.at[group]).start()
    root_copies = [
        pltpu.make_async_copy(
            line_ref.at[:, pl.ds(LEAF_ROWS, 8), pl.ds(512 * half, 512)],
            root_buffer.at[:, pl.ds(8 * half, 8), :],
            root_sem.at[half],
        )
        for half in range(2)
    ]
    start_all(root_copies)

    def out_copies(group):
        offset = jnp.int32(OFFSETS[0])
        for at in range(1, 4):
            offset = jnp.where(group == at, OFFSETS[at], offset)
        sep = lax.rem(y + offset + 8, 4)
        return sep, [
            pltpu.make_async_copy(high_ref.at[sep], high_hbm.at[sep], out_sem.at[2 * group]),
            pltpu.make_async_copy(low_ref.at[sep], low_hbm.at[sep], out_sem.at[2 * group + 1]),
        ]

    def one_group(group, _):
        for _ in range(8):
            pltpu.make_async_copy(own_refs[0].at[0], buffer.at[0, 0, 0], sem.at[group]).wait()
        sep, copies = out_copies(group)

        def rows(parity, first, tiles):
            return jnp.concatenate([
                jnp.concatenate([buffer[sep, q, parity, first + tile] for tile in range(tiles)], axis=1)
                for q in range(4)
            ], axis=0)

        for z in range(8):
            width = TILES[z] * LANES
            for parity in range(2):
                first_row = 32 * (2 * z + parity)
                row_ids = first_row + lax.broadcasted_iota(jnp.int32, (32, width), 0)
                col_ids = lax.broadcasted_iota(jnp.int32, (32, width), 1)
                value = lower_unit(rows(parity, FIRST_TILE[z], TILES[z]), row_ids, col_ids)
                high, low = split2(value)
                to = slice(first_row, first_row + 32)
                high_ref[sep, to, :width] = high
                low_ref[sep, to, :width] = low
                if width < 512:
                    high_ref[sep, to, width:] = jnp.zeros((32, 512 - width), BF16)
                    low_ref[sep, to, width:] = jnp.zeros((32, 512 - width), BF16)

        def border_rows(z, _):
            for parity in range(2):
                to = pl.ds(pl.multiple_of((2 * z + parity) * 32, 32), 32)
                high_ref[sep, to], low_ref[sep, to] = split2(rows(parity, FIRST_TILE[8] + 4 * (z - 8), 4))
            return 0

        lax.fori_loop(8, 16, border_rows, 0)
        start_all(copies)
        return 0

    lax.fori_loop(0, 4, one_group, 0)
    wait_all(root_copies)
    row_ids = lax.broadcasted_iota(jnp.int32, (512, 512), 0)
    col_ids = lax.broadcasted_iota(jnp.int32, (512, 512), 1)
    value = lower_unit(root_buffer[...].reshape(512, 512), row_ids, col_ids)
    root_high_ref[...], root_low_ref[...] = split2(value)
    root_stores = [
        pltpu.make_async_copy(root_high_ref, root_high_hbm, out_sem.at[8]),
        pltpu.make_async_copy(root_low_ref, root_low_hbm, out_sem.at[9]),
    ]
    start_all(root_stores)
    for group in range(4):
        wait_all(out_copies(group)[1])
    wait_all(root_stores)


def lower_unit(value, row_ids, col_ids):
    return jnp.where(col_ids == row_ids, 1.0, jnp.where(col_ids < row_ids, value, 0.0))


def upper_operators(place, own, other, line):
    return pl.pallas_call(
        upper_operator_kernel,
        out_shape=(
            jax.ShapeDtypeStruct((4, 1024, 512), BF16),
            jax.ShapeDtypeStruct((4, 1024, 512), BF16),
            jax.ShapeDtypeStruct((512, 512), BF16),
            jax.ShapeDtypeStruct((512, 512), BF16),
        ),
        in_specs=[full_smem()] + [in_hbm()] * 9,
        out_specs=(in_hbm(),) * 4,
        scratch_shapes=[
            pltpu.VMEM((NY, NX, NC, PACKED, 8, LANES), F32),
            pltpu.VMEM((32, 16, 512), F32),
            pltpu.VMEM((4, 1024, 512), BF16),
            pltpu.VMEM((4, 1024, 512), BF16),
            pltpu.VMEM((512, 512), BF16),
            pltpu.VMEM((512, 512), BF16),
            pltpu.SemaphoreType.DMA((4,)),
            pltpu.SemaphoreType.DMA((2,)),
            pltpu.SemaphoreType.DMA((10,)),
        ],
        compiler_params=params(60),
        name="upper_operators",
    )(place, *own, *other, line)


def upper_kernel(
    parent_ref, incoming_ref, slot_ref, index_ref, sep_rhs_ref, sep_slot_ref, sep_index_ref, root_rhs_ref,
    high_hbm, low_hbm, root_high_hbm, root_low_hbm,
    down_ref, sep_out_ref, root_out_ref,
    updates, solved, full, high_ref, low_ref, root_high_ref, root_low_ref, sem,
):
    loads = []
    for sep in range(4):
        loads.append([
            pltpu.make_async_copy(high_hbm.at[sep], high_ref.at[sep], sem.at[sep, 0]),
            pltpu.make_async_copy(low_hbm.at[sep], low_ref.at[sep], sem.at[sep, 1]),
        ])
    loads.append([
        pltpu.make_async_copy(root_high_hbm, root_high_ref, sem.at[4, 0]),
        pltpu.make_async_copy(root_low_hbm, root_low_ref, sem.at[4, 1]),
    ])
    for group in loads:
        start_all(group)
    updates[...] = jnp.zeros(updates.shape, F32)

    def spread(leaf, _):
        to = parent_ref[leaf]
        picked = pick(blocks(incoming_ref[leaf]), slot_ref[leaf])
        for at, value in enumerate(picked):
            part = slice(at * LANES, (at + 1) * LANES)
            updates[to, :, part] = updates[to, :, part] + value
        return 0

    lax.fori_loop(0, 16, spread, 0, unroll=4)
    root_total = root_rhs_ref[...]
    for sep in range(4):
        wait_all(loads[sep])
        pivot = stack2(split2(sep_rhs_ref[sep] + updates[sep, :, :512]))
        forward = stacked_products(dot_nt, pivot, (high_ref[sep], low_ref[sep]))
        solved[sep] = forward[:, :512]
        border = forward[:, 512:] + updates[sep, :, 512:]
        root_total = root_total + jnp.concatenate(pick(blocks(border), sep_slot_ref[sep]), axis=1)
    wait_all(loads[4])
    root = (root_high_ref[...], root_low_ref[...])
    root_solved = stacked_products(dot_nt, stack2(split2(root_total)), root)
    root_answer = stacked_products(dot_nn, stack2(split2(root_solved)), root)
    root_out_ref[...] = root_answer
    for sep in range(4):
        border = jnp.concatenate(pick(blocks(root_answer), sep_index_ref[sep]), axis=1)
        joined = stack2(split2(jnp.concatenate([solved[sep], border], axis=1)))
        answer = stacked_products(dot_nn, joined, (high_ref[sep], low_ref[sep]))
        sep_out_ref[sep] = answer
        full[sep, :, :512] = answer
        full[sep, :, 512:] = border

    def gather(leaf, _):
        picked = pick(blocks(full[parent_ref[leaf]]), index_ref[leaf])
        down_ref[leaf] = jnp.concatenate(picked, axis=1)
        return 0

    lax.fori_loop(0, 16, gather, 0, unroll=4)


def upper_solve(parent, incoming, slots, index, sep_rhs, sep_slots, sep_index, root_rhs, operators):
    return pl.pallas_call(
        upper_kernel,
        out_shape=(
            jax.ShapeDtypeStruct((16, 16, 512), F32),
            jax.ShapeDtypeStruct((4, 16, 512), F32),
            jax.ShapeDtypeStruct((16, 512), F32),
        ),
        in_specs=[full_smem()] + [full_vmem()] * 7 + [in_hbm()] * 4,
        out_specs=(full_vmem(),) * 3,
        scratch_shapes=[
            pltpu.VMEM((4, 16, 1024), F32),
            pltpu.VMEM((4, 16, 512), F32),
            pltpu.VMEM((4, 16, 1024), F32),
            pltpu.VMEM((4, 1024, 512), BF16),
            pltpu.VMEM((4, 1024, 512), BF16),
            pltpu.VMEM((512, 512), BF16),
            pltpu.VMEM((512, 512), BF16),
            pltpu.SemaphoreType.DMA((5, 2)),
        ],
        compiler_params=params(60),
        name="upper_solve",
    )(parent, incoming, slots, index, sep_rhs, sep_slots, sep_index, root_rhs, *operators)


def inverse_rows(index, extent):
    place = jnp.arange(index.shape[1], dtype=jnp.int32)[None, :, None]
    slot = jnp.arange(extent, dtype=jnp.int32)[None, None, :]
    return jnp.max(jnp.where(index[:, :, None] == slot, place, -1), axis=1)


def swap_cores(value):
    return lax.ppermute(value, "c", [(0, 1), (1, 0)])


def along_plane(value, step, first):
    pairs = []
    for y in range(NY):
        for x in range(NX):
            for c in range(NC):
                by_x = (c == 0) == first
                to_y, to_x = (y, (x + step) % NX) if by_x else ((y + step) % NY, x)
                pairs.append(((y * NX + x) * NC + c, (to_y * NX + to_x) * NC + c))
    return lax.ppermute(value, ("y", "x", "c"), pairs)


def gather_line(separator_factor, y, x):
    mine = lax.dynamic_slice(separator_factor, (y, 8 * x, 0), (1, 8, 512))
    return lax.all_to_all(
        jnp.broadcast_to(mine, (NZ, 8, 512)), "z", split_axis=0, concat_axis=0, tiled=True
    )


def spread_line(line):
    rows = jnp.stack([line, along_plane(line, 1, True), along_plane(line, -1, True), along_plane(line, 2, True)])
    ahead, back = along_plane(rows, 1, False), along_plane(rows, -1, False)
    own = (rows, ahead, back, along_plane(ahead, 1, False))
    return own, tuple(swap_cores(part) for part in own)


def local(
    leaf_rhs,
    leaf_factor,
    pivot_count,
    parent,
    leaf_index,
    separator_rhs,
    separator_factor,
    separator_index,
    root_rhs,
    root_factor,
):
    rhs = leaf_rhs[0]
    slots = inverse_rows(leaf_index, 1024)[:, None, :]
    sep_slots = inverse_rows(separator_index, 512)[:, None, :]
    sep_rhs = jnp.transpose(separator_rhs[0], (1, 0, 2))
    y, x, c = lax.axis_index("y"), lax.axis_index("x"), lax.axis_index("c")
    place = jnp.stack([y, x, c]).astype(jnp.int32)
    line = lax.all_gather(join(leaf_factor[0], root_factor), ("z", "c"), axis=0, tiled=False)
    sep_line = gather_line(separator_factor, y, x)
    sep_line, slots, sep_slots, sep_rhs = lax.optimization_barrier((sep_line, slots, sep_slots, sep_rhs))
    own_set, other_set = spread_line(pack(sep_line))
    border = leaf_border(pivot_count, rhs, line)
    line, border = lax.optimization_barrier((line, border))
    incoming = lax.all_to_all(
        border.reshape(16, 16, 512), ("y", "x"), split_axis=0, concat_axis=0, tiled=True
    )
    operators = upper_operators(place, own_set, other_set, line)
    down, sep_answer, root_answer = upper_solve(
        parent, incoming, slots, leaf_index[:, None, :], sep_rhs, sep_slots,
        separator_index[:, None, :], root_rhs[0], operators,
    )
    line, down = lax.optimization_barrier((line, down))
    received = lax.all_to_all(down, ("y", "x"), split_axis=0, concat_axis=0, tiled=True)
    part, high, low = leaf_pivot(pivot_count, rhs, line)
    leaf_answer = leaf_last(pivot_count, part, received.reshape(256, 512), high, low)
    return leaf_answer[None], jnp.transpose(sep_answer, (1, 0, 2))[None], root_answer[None]


def solution(mesh):
    fine = Mesh(mesh.devices.reshape(NY, NX, NZ, NC), ("y", "x", "z", "c"))
    leaf, src = ("y", "x"), ("z", "c")
    return jax.shard_map(
        local,
        mesh=fine,
        in_specs=(
            P(leaf, src, None),
            P(leaf, src, None),
            P(leaf),
            P(),
            P(),
            P(leaf, src, None, None),
            P(None, src, None),
            P(),
            P(leaf, src, None),
            P(src, None),
        ),
        out_specs=(P(leaf, src, None), P(leaf, src, None, None), P(leaf, src, None)),
        check_vma=False,
    )
```

```python
import jax
import jax.numpy as jnp
from jax import lax
from jax.experimental import pallas as pl
from jax.experimental.pallas import tpu as pltpu
from jax.sharding import Mesh, PartitionSpec as P

NY, NX, NZ, NC = 4, 4, 16, 2
F32, BF16 = jnp.float32, jnp.bfloat16
LANES = 128


def split2(value):
    high = value.astype(BF16)
    return high, (value - high.astype(F32)).astype(BF16)


def dot_nt(a, b):
    return lax.dot_general(a, b, (((1,), (1,)), ((), ())), preferred_element_type=F32)


def dot_nn(a, b):
    return lax.dot_general(a, b, (((1,), (0,)), ((), ())), preferred_element_type=F32)


def stack2(pair):
    return jnp.concatenate(pair, axis=0)


def stacked_products(dot, both, b):
    rows = both.shape[0] // 2
    first = dot(both, b[0])
    return first[:rows] + (first[rows:] + dot(both[:rows], b[1]))


def params(mebibytes):
    return pltpu.CompilerParams(vmem_limit_bytes=mebibytes * 1024 * 1024)


def full_vmem():
    return pl.BlockSpec(memory_space=pltpu.VMEM)


def full_smem():
    return pl.BlockSpec(memory_space=pltpu.SMEM)


def in_hbm():
    return pl.BlockSpec(memory_space=pltpu.HBM)


def anywhere():
    return pl.BlockSpec(memory_space=pl.ANY)


def start_all(copies):
    for copy in copies:
        copy.start()


def wait_all(copies):
    for copy in copies:
        copy.wait()


LEAF_ROWS, SHARD = 48, 56


def join_kernel(leaf_ref, root_ref, out_ref):
    out_ref[:LEAF_ROWS] = leaf_ref[...]
    out_ref[LEAF_ROWS:, :512] = root_ref[:8]
    out_ref[LEAF_ROWS:, 512:] = root_ref[8:]


def join(leaf, root):
    return pl.pallas_call(
        join_kernel,
        out_shape=jax.ShapeDtypeStruct((SHARD, 1024), F32),
        in_specs=[full_vmem()] * 2,
        out_specs=full_vmem(),
        compiler_params=params(60),
        name="join",
    )(leaf, root)


def leaf_copy(line_ref, buffer, first, count, sem):
    return pltpu.make_async_copy(line_ref.at[pl.ds(first, count), pl.ds(0, LEAF_ROWS), :], buffer, sem)


def leaf_border_kernel(count_ref, rhs_hbm, line_ref, border_ref, rhs_ref, buffer, sem, rhs_sem):
    copy = leaf_copy(line_ref, buffer, 21, 11, sem)
    load = pltpu.make_async_copy(rhs_hbm, rhs_ref, rhs_sem)
    load.start()
    copy.start()
    load.wait()
    cols = lax.broadcasted_iota(jnp.int32, rhs_ref.shape, 1)
    rhs = stack2(split2(jnp.where(cols < count_ref[0], rhs_ref[...], 0.0)))
    copy.wait()
    rows = buffer[...].reshape(528, 1024)
    for block in range(2):
        first = 16 + 256 * block
        border_ref[:, 256 * block : 256 * (block + 1)] = stacked_products(
            dot_nt, rhs, split2(rows[first : first + 256])
        )


def leaf_border(count, rhs, line):
    return pl.pallas_call(
        leaf_border_kernel,
        out_shape=jax.ShapeDtypeStruct((256, 512), F32),
        in_specs=[full_smem(), in_hbm(), in_hbm()],
        out_specs=full_vmem(),
        scratch_shapes=[
            pltpu.VMEM((256, 1024), F32),
            pltpu.VMEM((11, 48, 1024), F32),
            pltpu.SemaphoreType.DMA,
            pltpu.SemaphoreType.DMA,
        ],
        compiler_params=params(60),
        name="leaf_border",
    )(count, rhs, line)


def leaf_pivot_kernel(
    count_ref, rhs_hbm, line_ref,
    part_hbm, border_high_hbm, border_low_hbm,
    rhs_ref, buffer, border_buffer, high_ref, low_ref, part_ref, border_high_ref, border_low_ref, sem, out_sem,
):
    copy = leaf_copy(line_ref, buffer, 0, 22, sem.at[0])
    border_copy = leaf_copy(line_ref, border_buffer, 21, 11, sem.at[1])
    load = pltpu.make_async_copy(rhs_hbm, rhs_ref, sem.at[2])
    load.start()
    copy.start()
    border_copy.start()
    count = count_ref[0]
    load.wait()
    cols = lax.broadcasted_iota(jnp.int32, rhs_ref.shape, 1)
    rhs = stack2(split2(jnp.where(cols < count, rhs_ref[...], 0.0)))
    copy.wait()
    top = buffer[...].reshape(1056, 1024)
    solved = []
    for block in range(4):
        first, wide = 256 * block, 256 * (block + 1)
        rows = first + lax.broadcasted_iota(jnp.int32, (256, wide), 0)
        columns = lax.broadcasted_iota(jnp.int32, (256, wide), 1)
        values = jnp.where(columns < rows, top[first:wide, :wide], 0.0)
        values = jnp.where(columns == rows, 1.0, values)
        values = jnp.where(rows < count, values, 0.0)
        high, low = split2(values)
        high_ref[first:wide, :wide] = high
        low_ref[first:wide, :wide] = low
        solved.append(stacked_products(dot_nt, rhs[:, :wide], (high, low)))
    solved = stack2(split2(jnp.concatenate(solved, axis=1)))
    border_copy.wait()
    border = border_buffer[...].reshape(528, 1024)
    stores = []
    for block in range(4):
        first, wide = 256 * block, 256 * (block + 1)
        border_high_ref[block], border_low_ref[block] = split2(border[16:, first:wide])
        part_ref[block] = stacked_products(
            dot_nn,
            solved[:, first:],
            (high_ref[first:, first:wide], low_ref[first:, first:wide]),
        )
        stores += [
            pltpu.make_async_copy(part_ref.at[block], part_hbm.at[block], out_sem.at[block, 0]),
            pltpu.make_async_copy(border_high_ref.at[block], border_high_hbm.at[block], out_sem.at[block, 1]),
            pltpu.make_async_copy(border_low_ref.at[block], border_low_hbm.at[block], out_sem.at[block, 2]),
        ]
        start_all(stores[-3:])
    wait_all(stores)


def leaf_pivot(count, rhs, line):
    return pl.pallas_call(
        leaf_pivot_kernel,
        out_shape=(
            jax.ShapeDtypeStruct((4, 256, 256), F32),
            jax.ShapeDtypeStruct((4, 512, 256), BF16),
            jax.ShapeDtypeStruct((4, 512, 256), BF16),
        ),
        in_specs=[full_smem(), in_hbm(), in_hbm()],
        out_specs=(in_hbm(),) * 3,
        scratch_shapes=[
            pltpu.VMEM((256, 1024), F32),
            pltpu.VMEM((22, 48, 1024), F32),
            pltpu.VMEM((11, 48, 1024), F32),
            pltpu.VMEM((1024, 1024), BF16),
            pltpu.VMEM((1024, 1024), BF16),
            pltpu.VMEM((4, 256, 256), F32),
            pltpu.VMEM((4, 512, 256), BF16),
            pltpu.VMEM((4, 512, 256), BF16),
            pltpu.SemaphoreType.DMA((3,)),
            pltpu.SemaphoreType.DMA((4, 3)),
        ],
        compiler_params=params(60),
        name="leaf_pivot",
    )(count, rhs, line)


def leaf_last_kernel(
    count_ref, part_hbm, border_ref, high_hbm, low_hbm, out_hbm,
    part_ref, high_ref, low_ref, out_ref, sem, out_sem,
):
    copies = [
        [
            pltpu.make_async_copy(source.at[block], to.at[block], sem.at[block, at])
            for at, (source, to) in enumerate(((high_hbm, high_ref), (low_hbm, low_ref), (part_hbm, part_ref)))
        ]
        for block in range(4)
    ]
    for group in copies:
        start_all(group)
    border = stack2(split2(border_ref[...]))
    stores = []
    for block in range(4):
        wait_all(copies[block])
        answer = part_ref[block] + stacked_products(dot_nn, border, (high_ref[block], low_ref[block]))
        cols = 256 * block + lax.broadcasted_iota(jnp.int32, answer.shape, 1)
        out_ref[block] = jnp.where(cols < count_ref[0], answer, 0.0)
        stores.append(
            pltpu.make_async_copy(out_ref.at[block], out_hbm.at[:, pl.ds(256 * block, 256)], out_sem.at[block])
        )
        stores[-1].start()
    wait_all(stores)


def leaf_last(count, part, border, high, low):
    return pl.pallas_call(
        leaf_last_kernel,
        out_shape=jax.ShapeDtypeStruct((256, 1024), F32),
        in_specs=[full_smem(), in_hbm(), full_vmem(), in_hbm(), in_hbm()],
        out_specs=in_hbm(),
        scratch_shapes=[
            pltpu.VMEM((4, 256, 256), F32),
            pltpu.VMEM((4, 512, 256), BF16),
            pltpu.VMEM((4, 512, 256), BF16),
            pltpu.VMEM((4, 256, 256), F32),
            pltpu.SemaphoreType.DMA((4, 3)),
            pltpu.SemaphoreType.DMA((4,)),
        ],
        compiler_params=params(59),
        name="leaf_last",
    )(count, part, border, high, low)


LANE_GATHER = lax.GatherDimensionNumbers(
    offset_dims=(),
    collapsed_slice_dims=(1,),
    start_index_map=(1,),
    operand_batching_dims=(0,),
    start_indices_batching_dims=(0,),
)


def take_lanes(value, lane):
    return lax.gather(
        value, lane[..., None], LANE_GATHER, slice_sizes=(1, 1), mode=lax.GatherScatterMode.PROMISE_IN_BOUNDS
    )


def pick(values, index_row):
    out = []
    for block in range(index_row.shape[1] // LANES):
        index = jnp.broadcast_to(index_row[:, block * LANES : (block + 1) * LANES], (8, LANES))
        lane, found = index & (LANES - 1), index >= 0
        bits = [(index & (LANES << bit)) != 0 for bit in range(len(values).bit_length() - 1)]
        halves = []
        for half in range(2):
            level = [take_lanes(value[8 * half : 8 * half + 8], lane) for value in values]
            for bit in bits:
                level = [jnp.where(bit, odd, even) for even, odd in zip(level[::2], level[1::2])]
            halves.append(jnp.where(found, level[0], 0.0))
        out.append(jnp.concatenate(halves, axis=0))
    return out


def blocks(value):
    return [value[:, at * LANES : (at + 1) * LANES] for at in range(value.shape[1] // LANES)]


OFFSETS = (0, -1, 1, -2)
TILES = [min(4, z // 2 + 1) for z in range(NZ)]
FIRST_TILE = [sum(TILES[:z]) for z in range(NZ)]
PACKED = sum(TILES)


def pack_kernel(line_ref, out_ref):
    for z in range(NZ):
        for tile in range(TILES[z]):
            out_ref[FIRST_TILE[z] + tile] = line_ref[z, :, tile * LANES : (tile + 1) * LANES]


def pack(line):
    return pl.pallas_call(
        pack_kernel,
        out_shape=jax.ShapeDtypeStruct((PACKED, 8, LANES), F32),
        in_specs=[full_vmem()],
        out_specs=full_vmem(),
        compiler_params=params(60),
        name="pack",
    )(line)


def upper_operator_kernel(place_ref, *refs):
    own_refs, other_refs, line_ref = refs[:4], refs[4:8], refs[8]
    high_hbm, low_hbm, root_high_hbm, root_low_hbm = refs[9:13]
    buffer, root_buffer, high_ref, low_ref, root_high_ref, root_low_ref, sem, root_sem, out_sem = refs[13:]
    y, x, c = place_ref[0], place_ref[1], place_ref[2]
    for piece_refs, parity in ((own_refs, c), (other_refs, 1 - c)):
        for outer in range(4):
            for inner in range(4):
                source = piece_refs[outer].at[inner]
                along_y = jnp.where(parity == 0, OFFSETS[outer], OFFSETS[inner])
                along_x = jnp.where(parity == 0, OFFSETS[inner], OFFSETS[outer])
                group = jnp.where(parity == 0, outer, inner)
                to_y = lax.rem(y + along_y + 8, 4)
                to_x = lax.rem(x + along_x + 8, 4)
                pltpu.make_async_copy(source, buffer.at[to_y, to_x, parity], sem.at[group]).start()
    root_copies = [
        pltpu.make_async_copy(
            line_ref.at[:, pl.ds(LEAF_ROWS, 8), pl.ds(512 * half, 512)],
            root_buffer.at[:, pl.ds(8 * half, 8), :],
            root_sem.at[half],
        )
        for half in range(2)
    ]
    start_all(root_copies)

    def out_copies(group):
        offset = jnp.int32(OFFSETS[0])
        for at in range(1, 4):
            offset = jnp.where(group == at, OFFSETS[at], offset)
        sep = lax.rem(y + offset + 8, 4)
        return sep, [
            pltpu.make_async_copy(high_ref.at[sep], high_hbm.at[sep], out_sem.at[2 * group]),
            pltpu.make_async_copy(low_ref.at[sep], low_hbm.at[sep], out_sem.at[2 * group + 1]),
        ]

    def one_group(group, _):
        for _ in range(8):
            pltpu.make_async_copy(own_refs[0].at[0], buffer.at[0, 0, 0], sem.at[group]).wait()
        sep, copies = out_copies(group)

        def rows(parity, first, tiles):
            return jnp.concatenate([
                jnp.concatenate([buffer[sep, q, parity, first + tile] for tile in range(tiles)], axis=1)
                for q in range(4)
            ], axis=0)

        for z in range(8):
            width = TILES[z] * LANES
            for parity in range(2):
                first_row = 32 * (2 * z + parity)
                row_ids = first_row + lax.broadcasted_iota(jnp.int32, (32, width), 0)
                col_ids = lax.broadcasted_iota(jnp.int32, (32, width), 1)
                value = lower_unit(rows(parity, FIRST_TILE[z], TILES[z]), row_ids, col_ids)
                high, low = split2(value)
                to = slice(first_row, first_row + 32)
                high_ref[sep, to, :width] = high
                low_ref[sep, to, :width] = low
                if width < 512:
                    high_ref[sep, to, width:] = jnp.zeros((32, 512 - width), BF16)
                    low_ref[sep, to, width:] = jnp.zeros((32, 512 - width), BF16)

        def border_rows(z, _):
            for parity in range(2):
                to = pl.ds(pl.multiple_of((2 * z + parity) * 32, 32), 32)
                high_ref[sep, to], low_ref[sep, to] = split2(rows(parity, FIRST_TILE[8] + 4 * (z - 8), 4))
            return 0

        lax.fori_loop(8, 16, border_rows, 0)
        start_all(copies)
        return 0

    lax.fori_loop(0, 4, one_group, 0)
    wait_all(root_copies)
    row_ids = lax.broadcasted_iota(jnp.int32, (512, 512), 0)
    col_ids = lax.broadcasted_iota(jnp.int32, (512, 512), 1)
    value = lower_unit(root_buffer[...].reshape(512, 512), row_ids, col_ids)
    root_high_ref[...], root_low_ref[...] = split2(value)
    root_stores = [
        pltpu.make_async_copy(root_high_ref, root_high_hbm, out_sem.at[8]),
        pltpu.make_async_copy(root_low_ref, root_low_hbm, out_sem.at[9]),
    ]
    start_all(root_stores)
    for group in range(4):
        wait_all(out_copies(group)[1])
    wait_all(root_stores)


def lower_unit(value, row_ids, col_ids):
    return jnp.where(col_ids == row_ids, 1.0, jnp.where(col_ids < row_ids, value, 0.0))


def upper_operators(place, own, other, line):
    return pl.pallas_call(
        upper_operator_kernel,
        out_shape=(
            jax.ShapeDtypeStruct((4, 1024, 512), BF16),
            jax.ShapeDtypeStruct((4, 1024, 512), BF16),
            jax.ShapeDtypeStruct((512, 512), BF16),
            jax.ShapeDtypeStruct((512, 512), BF16),
        ),
        in_specs=[full_smem()] + [in_hbm()] * 9,
        out_specs=(in_hbm(),) * 4,
        scratch_shapes=[
            pltpu.VMEM((NY, NX, NC, PACKED, 8, LANES), F32),
            pltpu.VMEM((32, 16, 512), F32),
            pltpu.VMEM((4, 1024, 512), BF16),
            pltpu.VMEM((4, 1024, 512), BF16),
            pltpu.VMEM((512, 512), BF16),
            pltpu.VMEM((512, 512), BF16),
            pltpu.SemaphoreType.DMA((4,)),
            pltpu.SemaphoreType.DMA((2,)),
            pltpu.SemaphoreType.DMA((10,)),
        ],
        compiler_params=params(60),
        name="upper_operators",
    )(place, *own, *other, line)


def upper_kernel(
    parent_ref, incoming_ref, slot_ref, index_ref, sep_rhs_ref, sep_slot_ref, sep_index_ref, root_rhs_ref,
    high_hbm, low_hbm, root_high_hbm, root_low_hbm,
    down_ref, sep_out_ref, root_out_ref,
    updates, solved, full, high_ref, low_ref, root_high_ref, root_low_ref, sem,
):
    loads = []
    for sep in range(4):
        loads.append([
            pltpu.make_async_copy(high_hbm.at[sep], high_ref.at[sep], sem.at[sep, 0]),
            pltpu.make_async_copy(low_hbm.at[sep], low_ref.at[sep], sem.at[sep, 1]),
        ])
    loads.append([
        pltpu.make_async_copy(root_high_hbm, root_high_ref, sem.at[4, 0]),
        pltpu.make_async_copy(root_low_hbm, root_low_ref, sem.at[4, 1]),
    ])
    for group in loads:
        start_all(group)
    updates[...] = jnp.zeros(updates.shape, F32)

    def spread(leaf, _):
        to = parent_ref[leaf]
        picked = pick(blocks(incoming_ref[leaf]), slot_ref[leaf])
        for at, value in enumerate(picked):
            part = slice(at * LANES, (at + 1) * LANES)
            updates[to, :, part] = updates[to, :, part] + value
        return 0

    lax.fori_loop(0, 16, spread, 0, unroll=4)
    root_total = root_rhs_ref[...]
    for sep in range(4):
        wait_all(loads[sep])
        pivot = stack2(split2(sep_rhs_ref[sep] + updates[sep, :, :512]))
        forward = stacked_products(dot_nt, pivot, (high_ref[sep], low_ref[sep]))
        solved[sep] = forward[:, :512]
        border = forward[:, 512:] + updates[sep, :, 512:]
        root_total = root_total + jnp.concatenate(pick(blocks(border), sep_slot_ref[sep]), axis=1)
    wait_all(loads[4])
    root = (root_high_ref[...], root_low_ref[...])
    root_solved = stacked_products(dot_nt, stack2(split2(root_total)), root)
    root_answer = stacked_products(dot_nn, stack2(split2(root_solved)), root)
    root_out_ref[...] = root_answer
    for sep in range(4):
        border = jnp.concatenate(pick(blocks(root_answer), sep_index_ref[sep]), axis=1)
        joined = stack2(split2(jnp.concatenate([solved[sep], border], axis=1)))
        answer = stacked_products(dot_nn, joined, (high_ref[sep], low_ref[sep]))
        sep_out_ref[sep] = answer
        full[sep, :, :512] = answer
        full[sep, :, 512:] = border

    def gather(leaf, _):
        picked = pick(blocks(full[parent_ref[leaf]]), index_ref[leaf])
        down_ref[leaf] = jnp.concatenate(picked, axis=1)
        return 0

    lax.fori_loop(0, 16, gather, 0, unroll=4)


def upper_solve(parent, incoming, slots, index, sep_rhs, sep_slots, sep_index, root_rhs, operators):
    return pl.pallas_call(
        upper_kernel,
        out_shape=(
            jax.ShapeDtypeStruct((16, 16, 512), F32),
            jax.ShapeDtypeStruct((4, 16, 512), F32),
            jax.ShapeDtypeStruct((16, 512), F32),
        ),
        in_specs=[full_smem()] + [full_vmem()] * 7 + [in_hbm()] * 4,
        out_specs=(full_vmem(),) * 3,
        scratch_shapes=[
            pltpu.VMEM((4, 16, 1024), F32),
            pltpu.VMEM((4, 16, 512), F32),
            pltpu.VMEM((4, 16, 1024), F32),
            pltpu.VMEM((4, 1024, 512), BF16),
            pltpu.VMEM((4, 1024, 512), BF16),
            pltpu.VMEM((512, 512), BF16),
            pltpu.VMEM((512, 512), BF16),
            pltpu.SemaphoreType.DMA((5, 2)),
        ],
        compiler_params=params(60),
        name="upper_solve",
    )(parent, incoming, slots, index, sep_rhs, sep_slots, sep_index, root_rhs, *operators)


def inverse_rows(index, extent):
    place = jnp.arange(index.shape[1], dtype=jnp.int32)[None, :, None]
    slot = jnp.arange(extent, dtype=jnp.int32)[None, None, :]
    return jnp.max(jnp.where(index[:, :, None] == slot, place, -1), axis=1)


def swap_cores(value):
    return lax.ppermute(value, "c", [(0, 1), (1, 0)])


def along_plane(value, step, first):
    pairs = []
    for y in range(NY):
        for x in range(NX):
            for c in range(NC):
                by_x = (c == 0) == first
                to_y, to_x = (y, (x + step) % NX) if by_x else ((y + step) % NY, x)
                pairs.append(((y * NX + x) * NC + c, (to_y * NX + to_x) * NC + c))
    return lax.ppermute(value, ("y", "x", "c"), pairs)


def gather_line(separator_factor, y, x):
    mine = lax.dynamic_slice(separator_factor, (y, 8 * x, 0), (1, 8, 512))
    return lax.all_to_all(
        jnp.broadcast_to(mine, (NZ, 8, 512)), "z", split_axis=0, concat_axis=0, tiled=True
    )


def spread_line(line):
    rows = jnp.stack([line, along_plane(line, 1, True), along_plane(line, -1, True), along_plane(line, 2, True)])
    ahead, back = along_plane(rows, 1, False), along_plane(rows, -1, False)
    return rows, ahead, back, along_plane(ahead, 1, False)


def local(
    leaf_rhs,
    leaf_factor,
    pivot_count,
    parent,
    leaf_index,
    separator_rhs,
    separator_factor,
    separator_index,
    root_rhs,
    root_factor,
):
    rhs = leaf_rhs[0]
    slots = inverse_rows(leaf_index, 1024)[:, None, :]
    sep_slots = inverse_rows(separator_index, 512)[:, None, :]
    sep_rhs = jnp.transpose(separator_rhs[0], (1, 0, 2))
    y, x, c = lax.axis_index("y"), lax.axis_index("x"), lax.axis_index("c")
    place = jnp.stack([y, x, c]).astype(jnp.int32)
    line = lax.all_gather(join(leaf_factor[0], root_factor), ("z", "c"), axis=0, tiled=False)
    sep_line = gather_line(separator_factor, y, x)
    sep_line, slots, sep_slots, sep_rhs = lax.optimization_barrier((sep_line, slots, sep_slots, sep_rhs))
    own_set = spread_line(pack(sep_line))
    other_set = tuple(swap_cores(part) for part in own_set[:3])
    border = leaf_border(pivot_count, rhs, line)
    far, line, border = lax.optimization_barrier((own_set[3], line, border))
    own_set, other_set = own_set[:3] + (far,), other_set + (swap_cores(far),)
    incoming = lax.all_to_all(
        border.reshape(16, 16, 512), ("y", "x"), split_axis=0, concat_axis=0, tiled=True
    )
    operators = upper_operators(place, own_set, other_set, line)
    down, sep_answer, root_answer = upper_solve(
        parent, incoming, slots, leaf_index[:, None, :], sep_rhs, sep_slots,
        separator_index[:, None, :], root_rhs[0], operators,
    )
    line, down = lax.optimization_barrier((line, down))
    received = lax.all_to_all(down, ("y", "x"), split_axis=0, concat_axis=0, tiled=True)
    part, high, low = leaf_pivot(pivot_count, rhs, line)
    leaf_answer = leaf_last(pivot_count, part, received.reshape(256, 512), high, low)
    return leaf_answer[None], jnp.transpose(sep_answer, (1, 0, 2))[None], root_answer[None]


def solution(mesh):
    fine = Mesh(mesh.devices.reshape(NY, NX, NZ, NC), ("y", "x", "z", "c"))
    leaf, src = ("y", "x"), ("z", "c")
    return jax.shard_map(
        local,
        mesh=fine,
        in_specs=(
            P(leaf, src, None),
            P(leaf, src, None),
            P(leaf),
            P(),
            P(),
            P(leaf, src, None, None),
            P(None, src, None),
            P(),
            P(leaf, src, None),
            P(src, None),
        ),
        out_specs=(P(leaf, src, None), P(leaf, src, None, None), P(leaf, src, None)),
        check_vma=False,
    )
```
